512 devices in a mesh: gx: 16 (over x, y), gy: 8 (over z_lo), gz: 4 (over z_hi, core).
Axes of the slice: x: 4, y: 4, z: 16 (z_hi: 2, z_lo: 8; z = z_hi * 8 + z_lo), core: 2. Of those that a mesh axis runs over, the one named last changes fastest.
Arguments:
- fields: float32 [16, 192, 64, 512], P(None, 'gx', 'gy', 'gz'), may hold values from -6 to 6
- speeds: float32 [3, 16], replicated, may hold values from -1.5 to 1.5
- kinetics: float32 [16, 16], replicated, may hold values from -2 to 0.75
- block_rank: int32 [192], P('gx'), may hold values from 0 to 191, each once
- x_factor: float32 [192, 96], replicated, may hold values from -0.4375 to 0.4375
- y_factor: float32 [64, 64], P('gy'), may hold values from -0.75 to 0.75
- z_factor: float32 [512, 54], P('gz'), may hold values from -0.25 to 0.25
Outputs:
- fields_next: float32 [16, 192, 64, 512], P(None, 'gx', 'gy', 'gz')
- core: float32 [16, 96, 64, 54], P('gz', 'gx', 'gy')
The draws below stay inside these ranges and needn't reach their ends.
Inputs may be any that keep to these rules, and one draw needn't show every extreme that they name: block_rank is a permutation of the 192 x planes.
All inputs are finite; a program needn't handle non-finite values.
Results may differ from the reference program's by a relative error of at most 0.000098.
Values sent between devices are 32-bit elements; how exact they have to be, the bound alone decides.
A program may use at most 128 MiB of HBM per device.

```python
import jax
import jax.numpy as jnp
from jax import lax

VARS = 16
RX = 96
RY = 64
RZ = 54
NX = 192
NY = 64
NZ = 512


def draw_speeds(key, part):
    key_size = jax.random.fold_in(key, 11)
    key_sign = jax.random.fold_in(key, 12)
    lowest = 1.3
    magnitude = jax.random.uniform(key_size, (3, VARS), jnp.float32, lowest, 1.5)
    flips = jax.random.uniform(key_sign, (3, VARS), jnp.float32, 0.0, 1.0)
    signs = jnp.where(flips < 0.5, -1.0, 1.0).astype(jnp.float32)
    return (magnitude * signs).astype(jnp.float32)


def draw_kinetics(key, part):
    key_rates = jax.random.fold_in(key, 21)
    spread = jnp.clip(0.25 * jax.random.normal(key_rates, (VARS, VARS), jnp.float32), -0.75, 0.75)
    damping = -1.25 * jnp.eye(VARS, dtype=jnp.float32)
    return (damping + spread).astype(jnp.float32)


def level_of(stream_key, shape, shards, smallest, top_value):
    loudness = 1.0
    for dim, shards_of in shards:
        draws = jax.random.uniform(jax.random.fold_in(jax.random.fold_in(stream_key, 6), dim), (shards_of,), jnp.float32, smallest / len(shards), top_value / len(shards))
        loudness = loudness * jnp.repeat(jnp.exp(draws), shape[dim] // shards_of).reshape((-1,) + (1,) * (len(shape) - 1 - dim))
    return loudness


def normal_values(own_key, shape, scale, bound, cuts=(), kind=jnp.bfloat16):
    entries = scale * jax.random.normal(own_key, shape, jnp.float32)
    if cuts:
        entries = entries * level_of(own_key, shape, cuts, -0.22, 0.18)
    return jnp.clip(entries, -bound, bound).astype(kind)


def setup_inputs(seed: int = 0) -> dict:
    key_of = jax.random.split(jax.random.key(seed), 8)
    return {
        "fields": normal_values(key_of[0], (VARS, NX, NY, NZ), 1.0, 6.0, ((1, 16), (2, 8), (3, 4)), jnp.float32),
        "speeds": draw_speeds(jax.random.fold_in(key_of[7], 71), 0),
        "kinetics": draw_kinetics(jax.random.fold_in(key_of[7], 71), 0),
        "block_rank": jax.random.permutation(key_of[3], NX).astype(jnp.int32),
        "x_factor": normal_values(key_of[4], (NX, RX), NX ** -0.5, 0.4375, (), jnp.float32),
        "y_factor": normal_values(key_of[5], (NY, RY), NY ** -0.5, 0.75, ((0, 8),), jnp.float32),
        "z_factor": normal_values(key_of[6], (NZ, RZ), NZ ** -0.5, 0.25, ((0, 4),), jnp.float32),
    }


COEFFS = (0.8, -0.2, 4.0 / 105.0, -1.0 / 280.0)
TIME_STEP = 0.45


def tendency(padded, speeds, kinetics):
    extent = [padded.shape[1] - 8, padded.shape[2] - 8, padded.shape[3] - 8]

    def window(direction, offset):
        starts = [4, 4, 4]
        starts[direction] = starts[direction] + offset
        return padded[:, starts[0]:starts[0] + extent[0], starts[1]:starts[1] + extent[1], starts[2]:starts[2] + extent[2]]

    center = window(0, 0)
    result = jnp.einsum('vw,wxyz->vxyz', kinetics, center, precision=lax.Precision.HIGHEST)
    for direction in range(3):
        gradient = COEFFS[0] * (window(direction, 1) - window(direction, -1))
        for offset in range(2, 5):
            gradient = gradient + COEFFS[offset - 1] * (window(direction, offset) - window(direction, -offset))
        result = result - speeds[direction][:, None, None, None] * gradient
    return result


def padded_of(values):
    return jnp.pad(values, ((0, 0), (4, 4), (4, 4), (4, 4)))


def reference(fields, speeds, kinetics, block_rank, x_factor, y_factor, z_factor):
    section = fields + TIME_STEP * tendency(padded_of(fields), speeds, kinetics)
    fields_next = 0.5 * (fields + section + TIME_STEP * tendency(padded_of(section), speeds, kinetics))
    x_rows = x_factor[block_rank.astype(jnp.int32)]
    hp = lax.Precision.HIGHEST
    partial_z = jnp.einsum('vxyz,zc->vxyc', fields_next, z_factor, precision=hp)
    partial_x = jnp.einsum('vxyc,xa->vayc', partial_z, x_rows, precision=hp)
    core = jnp.einsum('vayc,yb->vabc', partial_x, y_factor, precision=hp)
    return fields_next, core
```

```python
import jax
import jax.numpy as jnp
from jax import lax
from jax.experimental import pallas as pl
from jax.experimental.pallas import tpu as pltpu
from jax.sharding import PartitionSpec as P

COEFFS = (0.8, -0.2, 4.0 / 105.0, -1.0 / 280.0)
TIME_STEP = 0.45
MESH = pl.DeviceIdType.MESH
f32, bf16 = jnp.float32, jnp.bfloat16
NN = (((1,), (0,)), ((), ()))
NT = (((1,), (1,)), ((), ()))
TN = (((0,), (0,)), ((), ()))


def dot(a, b, dims=NN):
    return lax.dot_general(a, b, dims, preferred_element_type=f32)


def split(a):
    high = a.astype(bf16)
    return high, (a - high.astype(f32)).astype(bf16)


def iota(shape, dim):
    return lax.broadcasted_iota(jnp.int32, shape, dim)


def onehot(mask):
    return jnp.where(mask, 1.0, 0.0).astype(bf16)


def stencil(offset):
    value = jnp.zeros(offset.shape, f32)
    for k, c in enumerate(COEFFS):
        value = jnp.where(offset == k + 1, c, value)
        value = jnp.where(offset == -k - 1, -c, value)
    return value


def quadrants(t):
    m, n = t.shape[0] // 2, t.shape[1] // 2
    return t[:m, :n] + (t[m:, :n] + t[:m, n:])


def halves(t):
    n = t.shape[1] // 2
    return t[:, :n] + t[:, n:]


def both(a):
    return jnp.concatenate(split(a), axis=1)


def kernel(
    f_ref, speeds_ref, kin_ref, rank_ref, xf_ref, yf_ref, zf_ref,
    next_ref, core_ref,
    FX, SX, YB, ZS, ZB, FN, PB, BR, QB, CT, RB, EU, FU, SB, GB, XR, XG, YT, YG, ZP,
    A2, D2, E2, SEL, Z2, X2, W2, SXR, SZR,
    load_sem, out_sem, own_sem, ysend, yrecv, zsend, zrecv, z0send, z0recv, xsend, xrecv,
    bsend, brecv, csend, crecv, esend, erecv, fsend, frecv, gsend, grecv,
    xrs, xrr, yrs, yrr,
):
    g, l, q = lax.axis_index("gx"), lax.axis_index("gy"), lax.axis_index("gz")
    h, k = q // 2, lax.rem(q, 2)
    ring = h * 8 + l
    partner = q + 1 - 2 * k

    def ring_device(r):
        return (g, lax.rem(r, 8), 2 * (r // 8) + k)

    def remote(src, dst, send, recv, device):
        return pltpu.make_async_remote_copy(
            src_ref=src, dst_ref=dst, send_sem=send, recv_sem=recv,
            device_id=device, device_id_type=MESH)

    def load(x):
        return pltpu.make_async_copy(f_ref.at[:, x], FX.at[4 + x], load_sem.at[x])

    def ycopy(s, d, p):
        X = (FX, SX)[s]
        rows = pl.ds(4 * d, 4)
        return remote(X.at[4 + p, :, rows], YB.at[s, p, :, rows], ysend.at[s, d, p],
                      yrecv.at[s, d, p], (g, l + 2 * d - 1, q))

    def z0copy(d):
        rows = pl.ds(4 * d, 4)
        return remote(ZS.at[0, :, rows], ZB.at[0, :, rows], z0send.at[d], z0recv.at[d],
                      (g, l, q + 2 * d - 1))

    def zcopy(d, p):
        rows = pl.ds(4 * d, 4)
        return remote(ZS.at[1, p, rows], ZB.at[1, p, rows], zsend.at[d, p], zrecv.at[d, p],
                      (g, l, q + 2 * d - 1))

    def xcopy(s, d, i):
        X = (FX, SX)[s]
        src, dst = (12 + i, i) if d else (4 + i, 16 + i)
        return remote(X.at[src], X.at[dst], xsend.at[s, d, i], xrecv.at[s, d, i],
                      (g + 2 * d - 1, l, q))

    def bcopy(x):
        return remote(PB.at[1 - k, x], BR.at[x], bsend.at[x], brecv.at[x], (g, l, partner))

    def can_send(index, last, d):
        return index < last if d else index > 0

    def can_recv(index, last, d):
        return index > 0 if d else index < last

    for x in range(12):
        load(x).start()

    barrier = pltpu.get_barrier_semaphore()

    def greet(device):
        pl.semaphore_signal(barrier, inc=1, device_id=device, device_id_type=MESH)

    far = jnp.logical_or(q == 1, q == 2)

    def greet_others(i, c):
        greet((lax.rem(g + i, 16), l, q))
        greet(ring_device(lax.rem(ring + i, 16)))
        return c

    greet((g, l, partner))
    lax.fori_loop(1, 16, greet_others, 0)

    @pl.when(far)
    def _():
        greet((g, l, 3 - q))

    for d in range(2):
        rows = pl.ds(4 * d, 4)

        @pl.when(jnp.logical_not(can_recv(l, 7, d)))
        def _():
            YB[:, :, :, rows, :] = jnp.zeros((2, 12, 16, 4, 128), f32)

        @pl.when(jnp.logical_not(can_recv(q, 3, d)))
        def _():
            ZB[:, :, rows, :] = jnp.zeros((2, 12, 4, 128), f32)

        @pl.when(jnp.logical_not(can_recv(g, 15, d)))
        def _():
            for X in (FX, SX):
                X[pl.ds(0 if d else 16, 4)] = jnp.zeros((4, 16, 8, 128), f32)

    i8, c8 = iota((8, 256), 0), jnp.bitwise_and(iota((8, 256), 1), 127)
    SEL[...] = onehot(c8 == jnp.where(i8 < 4, i8, 120 + i8))

    for x in range(12):
        load(x).wait()

    pl.semaphore_wait(barrier, 31 + jnp.where(far, 1, 0))

    def send_edges(j, c):
        for p in (5 - j, 6 + j):
            for d in range(2):
                pl.when(can_send(l, 7, d))(lambda: ycopy(0, d, p).start())
        return c

    def send_planes(i, c):
        pl.when(can_send(g, 15, 1))(lambda: xcopy(0, 1, 3 - i).start())
        pl.when(can_send(g, 15, 0))(lambda: xcopy(0, 0, i).start())
        return c

    lax.fori_loop(0, 2, send_edges, 0)
    lax.fori_loop(0, 4, send_planes, 0)
    lax.fori_loop(2, 6, send_edges, 0)

    def first_z(x, c):
        ZS[0, x] = dot(SEL[...], both(FX[4 + x].reshape(128, 128)), NT)
        return c

    lax.fori_loop(0, 12, first_z, 0)
    for d in range(2):
        pl.when(can_send(q, 3, d))(lambda: z0copy(d).start())

    row, col = iota((128, 256), 0), iota((128, 256), 1)
    v, y = row >> 3, jnp.bitwise_and(row, 7)
    own = col < 128
    cc = jnp.bitwise_and(col, 127)
    w, s8 = cc >> 3, jnp.bitwise_and(cc, 7)
    y2 = jnp.where(own, s8, jnp.where(s8 < 4, 8 + s8, s8 - 8))
    rows_v = onehot(iota((128, 16), 0) >> 3 == iota((128, 16), 1))
    cols_w = onehot(jnp.bitwise_and(iota((16, 256), 1), 127) >> 3 == iota((16, 256), 0))

    def spread(value):
        total = jnp.zeros((128, 256), f32)
        for part in split(value):
            total = total + dot(dot(rows_v, part).astype(bf16), cols_w)
        return total

    lane = iota((16, 16), 1) == iota((16, 16), 0)

    def speed_rows(d):
        total = jnp.zeros((128, 256), f32)
        for part in split(jnp.where(lane, speeds_ref[d : d + 1, :], 0.0)):
            total = total + dot(rows_v, dot(part, jnp.ones((16, 256), bf16)).astype(bf16))
        return -TIME_STEP * total

    SXR[...] = speed_rows(0)[:, :128]
    SZR[...] = speed_rows(2)[:, :128]
    A = jnp.where(y == y2, TIME_STEP * spread(kin_ref[...]), 0.0)
    A = A + jnp.where(v == w, speed_rows(1) * stencil(y2 - y), 0.0)
    A2[...] = jnp.concatenate(split(A), axis=0)
    D = both(stencil(iota((128, 128), 0) - iota((128, 128), 1)))
    D2[...] = jnp.concatenate([D, D], axis=0)
    i8, z8 = iota((8, 128), 0), iota((8, 128), 1)
    E = both(stencil(jnp.where(i8 < 4, 128 + i8, i8 - 8) - z8))
    E2[...] = jnp.concatenate([E, E], axis=0)
    ZP[...] = jnp.zeros((128, 128), f32)
    ZP[:, 0:54] = zf_ref[...]
    Z2[...] = both(jnp.concatenate([ZP[...], pltpu.roll(ZP[...], 64, 1)], axis=0))

    XR[...] = jnp.zeros((16, 128), f32)
    for x in range(12):
        XR[x : x + 1, 0:96] = xf_ref[pl.ds(rank_ref[x], 1), :]
    YT[...] = jnp.zeros((8, 128), f32)
    YT[:, 0:64] = yf_ref[...]
    XG[g] = XR[...]
    YG[l] = YT[...]

    def xrow(peer, slot):
        return remote(XR, XG.at[slot], xrs.at[peer], xrr.at[slot], (peer, l, q))

    def yrow(peer, slot):
        return remote(YT, YG.at[slot], yrs.at[peer], yrr.at[slot], (g, peer, q))

    def over(n, me, act):
        def body(i, c):
            act(lax.rem(me + i, n))
            return c
        lax.fori_loop(1, n, body, 0)

    over(16, g, lambda peer: xrow(peer, g).start())
    over(8, l, lambda peer: yrow(peer, l).start())

    def change(X, s, p):
        center = X[4 + p].reshape(128, 128)
        F = jnp.concatenate([both(center), both(YB[s, p].reshape(128, 128))], axis=0)
        t = dot(A2[...], F)
        zt = dot(F[:128], D2[...])
        zt = zt + dot(jnp.concatenate(split(ZB[s, p]), axis=0), E2[...], TN)
        xt = jnp.zeros((16, 8, 128), f32)
        for i, c in enumerate(COEFFS):
            xt = xt + c * (X[5 + i + p] - X[3 - i + p])
        return center, quadrants(t) + SZR[...] * halves(zt) + SXR[...] * xt.reshape(128, 128)

    def wait_halo(j, s):
        for p in (5 - j, 6 + j):
            for d in range(2):
                pl.when(can_recv(l, 7, d))(lambda: ycopy(s, d, p).wait_recv())
                if s:
                    pl.when(can_recv(q, 3, d))(lambda: zcopy(d, p).wait_recv())
        for d in range(2):
            i = 5 - j if d else j - 2
            pl.when(jnp.logical_and(j >= 2, can_recv(g, 15, d)))(
                lambda: xcopy(s, d, i).wait_recv())

    for d in range(2):
        pl.when(can_recv(q, 3, d))(lambda: z0copy(d).wait_recv())

    def first(j, c):
        wait_halo(j, 0)
        for p in (5 - j, 6 + j):
            center, add = change(FX, 0, p)
            section = center + add
            SX[4 + p] = section.reshape(16, 8, 128)
            for d in range(2):
                pl.when(can_send(l, 7, d))(lambda: ycopy(1, d, p).start())
            ZS[1, p] = dot(SEL[...], both(section), NT)
            for d in range(2):
                pl.when(can_send(q, 3, d))(lambda: zcopy(d, p).start())
        for d in range(2):
            i = j - 2 if d else 5 - j
            pl.when(jnp.logical_and(j >= 2, can_send(g, 15, d)))(
                lambda: xcopy(1, d, i).start())
        return c

    lax.fori_loop(0, 6, first, 0)

    over(16, g, lambda peer: xrow(peer, peer).wait_recv())
    over(8, l, lambda peer: yrow(peer, peer).wait_recv())
    shape = (4, 12, 8, 256)
    src = 4 * iota(shape, 0) + (iota(shape, 2) >> 1)
    pick = onehot((16 * src + iota(shape, 1) == iota(shape, 3)).reshape(384, 256))
    shape = (6, 4, 8, 128)
    rank = 24 * iota(shape, 1) + 6 * (iota(shape, 2) >> 1) + iota(shape, 0)
    ranks = onehot((rank == iota(shape, 3)).reshape(192, 128))
    same = jnp.bitwise_and(iota((192, 384), 0) ^ iota((192, 384), 1), 1) == 0
    for n, part in enumerate(split(XG[...].reshape(256, 128))):
        rows = dot(ranks, dot(pick, part).astype(bf16), NT)
        X2[192 * n : 192 * n + 192, :] = jnp.where(same, rows, 0.0).astype(bf16)
    Y = YG[...].reshape(64, 128)
    Y = Y + pltpu.roll(Y, 64, 1)
    col = iota((64, 256), 1)
    pick = onehot(8 * jnp.bitwise_and(col >> 4, 7) + jnp.bitwise_and(col, 7) == iota((64, 256), 0))
    same = iota((128, 256), 0) >> 6 == jnp.bitwise_and(iota((128, 256), 1) >> 3, 1)
    for n, part in enumerate(split(Y)):
        W2[128 * n : 128 * n + 128, :] = jnp.where(same, dot(part, pick, TN), 0.0).astype(bf16)

    def put(p):
        return pltpu.make_async_copy(FN.at[p], next_ref.at[:, p], out_sem.at[p])

    def second(j, c):
        wait_halo(j, 1)
        for p in (5 - j, 6 + j):
            center, add = change(SX, 1, p)
            new = 0.5 * (FX[4 + p].reshape(128, 128) + center + add)
            FN[p] = new.reshape(16, 8, 128)
            put(p).start()
            new = new.reshape(8, 2, 8, 128)
            pair = jnp.concatenate([new[:, 0].reshape(64, 128), new[:, 1].reshape(64, 128)], axis=1)
            z = quadrants(dot(jnp.concatenate(split(pair), axis=0), Z2[...]))
            z = z.reshape(2, 2, 2, 8, 128)
            for n in range(2):
                PB[n, p] = z[:, n].reshape(4, 8, 128)
            bcopy(p).start()
        return c

    lax.fori_loop(0, 6, second, 0)

    def add_partner(x, c):
        bcopy(x).wait_recv()
        QB[x] = PB[k, x] + BR[x]
        return c

    lax.fori_loop(0, 12, add_partner, 0)

    def place(d):
        return d // 4, pl.ds(2 * lax.rem(d, 4), 2)

    def ccopy(peer, slot):
        t, rows = place(peer)
        t2, rows2 = place(slot)
        return remote(QB.at[:, t, rows], CT.at[t2, :, rows2], csend.at[peer], crecv.at[slot],
                      (peer, l, q))

    def ecopy(peer, slot):
        t, rows = place(peer)
        t2, rows2 = place(slot)
        return remote(RB.at[:, t, rows], EU.at[t2, :, rows2], esend.at[peer], erecv.at[slot],
                      (peer, l, q))

    t, rows = place(g)
    over(16, g, lambda peer: ccopy(peer, g).start())
    mine = pltpu.make_async_copy(QB.at[:, t, rows], CT.at[t, :, rows], own_sem.at[0])
    mine.start()
    mine.wait()
    over(16, g, lambda peer: ccopy(peer, peer).wait_recv())
    R = quadrants(dot(X2[...], both(CT[...].reshape(384, 128))))
    RB[...] = R.reshape(6, 4, 8, 128)
    over(16, g, lambda peer: ecopy(peer, g).start())
    mine = pltpu.make_async_copy(RB.at[:, t, rows], EU.at[t, :, rows], own_sem.at[1])
    mine.start()
    mine.wait()
    over(16, g, lambda peer: ecopy(peer, peer).wait_recv())

    units = [(u, a, b) for u in range(2) for a in range(3) for b in range(2)]

    def fcopy(unit):
        u, a, b = unit
        return remote(EU.at[2 * b + u, pl.ds(2 * a, 2)], FU.at[ring], fsend.at[8 * b + 3 * u + a],
                      frecv.at[ring], (g, 1 + 3 * u + a, 2 * b + k))

    def fcome(r):
        return remote(EU.at[0, pl.ds(0, 2)], FU.at[r], fsend.at[0], frecv.at[r], ring_device(r))

    def to_self(unit):
        u, a, b = unit
        return jnp.logical_and(l == 1 + 3 * u + a, h == b)

    for unit in units:
        pl.when(jnp.logical_not(to_self(unit)))(lambda: fcopy(unit).start())

        @pl.when(to_self(unit))
        def _():
            u, a, b = unit
            FU[ring] = EU[2 * b + u, pl.ds(2 * a, 2)]

    def gcopy(there, slot):
        return remote(SB.at[:, there], GB.at[slot], gsend.at[there], grecv.at[slot], (g, there, q))

    works = jnp.logical_and(l >= 1, l <= 6)

    @pl.when(works)
    def _():
        over(16, ring, lambda r: fcome(r).wait_recv())
        S = quadrants(dot(W2[...], both(FU[...].reshape(256, 128))))
        SB[...] = S.reshape(2, 8, 8, 128)
        over(8, l, lambda there: gcopy(there, l - 1).start())
        GB[l - 1] = SB[:, l]

    for e in range(6):
        pl.when(l != e + 1)(lambda: gcopy(l, e).wait_recv())
    for u in range(2):
        for a in range(6):
            tile = GB[3 * u + a // 2, a % 2]
            core_ref[2 * u, a] = tile[:, 0:54]
            core_ref[2 * u + 1, a] = pltpu.roll(tile, 64, 1)[:, 0:54]

    def done(p, c):
        for s in range(2):
            for d in range(2):
                pl.when(can_send(l, 7, d))(lambda: ycopy(s, d, p).wait_send())
        for d in range(2):
            pl.when(can_send(q, 3, d))(lambda: zcopy(d, p).wait_send())
        bcopy(p).wait_send()
        put(p).wait()
        return c

    lax.fori_loop(0, 12, done, 0)
    for d in range(2):
        pl.when(can_send(q, 3, d))(lambda: z0copy(d).wait_send())
        for s in range(2):
            for i in range(4):
                pl.when(can_send(g, 15, d))(lambda: xcopy(s, d, i).wait_send())

    def done_peer(peer):
        xrow(peer, g).wait_send()
        ccopy(peer, g).wait_send()
        ecopy(peer, g).wait_send()

    over(16, g, done_peer)
    over(8, l, lambda peer: yrow(peer, l).wait_send())
    for unit in units:
        pl.when(jnp.logical_not(to_self(unit)))(lambda: fcopy(unit).wait_send())

    @pl.when(works)
    def _():
        over(8, l, lambda there: gcopy(there, l - 1).wait_send())


def local(fields, speeds, kinetics, block_rank, x_factor, y_factor, z_factor):
    vmem, dma = pltpu.VMEM, pltpu.SemaphoreType.DMA
    in_vmem = pl.BlockSpec(memory_space=pltpu.VMEM)
    anywhere = pl.BlockSpec(memory_space=pl.ANY)
    return pl.pallas_call(
        kernel,
        out_shape=(
            jax.ShapeDtypeStruct(fields.shape, f32),
            jax.ShapeDtypeStruct((4, 6, 8, 54), f32),
        ),
        in_specs=[anywhere, in_vmem, in_vmem, pl.BlockSpec(memory_space=pltpu.SMEM)] + [in_vmem] * 3,
        out_specs=(anywhere, in_vmem),
        scratch_shapes=[
            vmem((20, 16, 8, 128), f32),
            vmem((20, 16, 8, 128), f32),
            vmem((2, 12, 16, 8, 128), f32),
            vmem((2, 12, 8, 128), f32),
            vmem((2, 12, 8, 128), f32),
            vmem((12, 16, 8, 128), f32),
            vmem((2, 12, 4, 8, 128), f32),
            vmem((12, 4, 8, 128), f32),
            vmem((12, 4, 8, 128), f32),
            vmem((4, 12, 8, 128), f32),
            vmem((6, 4, 8, 128), f32),
            vmem((4, 6, 8, 128), f32),
            vmem((16, 2, 8, 128), f32),
            vmem((2, 8, 8, 128), f32),
            vmem((6, 2, 8, 128), f32),
            vmem((16, 128), f32),
            vmem((16, 16, 128), f32),
            vmem((8, 128), f32),
            vmem((8, 8, 128), f32),
            vmem((128, 128), f32),
            vmem((256, 256), bf16),
            vmem((256, 256), bf16),
            vmem((16, 256), bf16),
            vmem((8, 256), bf16),
            vmem((256, 256), bf16),
            vmem((384, 384), bf16),
            vmem((256, 256), bf16),
            vmem((128, 128), f32),
            vmem((128, 128), f32),
            dma((12,)), dma((12,)), dma((2,)),
            dma((2, 2, 12)), dma((2, 2, 12)),
            dma((2, 12)), dma((2, 12)), dma((2,)), dma((2,)),
            dma((2, 2, 4)), dma((2, 2, 4)),
            dma((12,)), dma((12,)),
            dma((16,)), dma((16,)), dma((16,)), dma((16,)), dma((16,)), dma((16,)),
            dma((8,)), dma((8,)),
            dma((16,)), dma((16,)), dma((8,)), dma((8,)),
        ],
        compiler_params=pltpu.CompilerParams(
            collective_id=0, has_side_effects=True, vmem_limit_bytes=32 * 1024 * 1024),
    )(fields, speeds, kinetics, block_rank, x_factor, y_factor, z_factor)


def solution(mesh):
    placed = (P(None, "gx", "gy", "gz"), P(), P(), P("gx"), P(), P("gy", None), P("gz", None))
    return jax.shard_map(
        local,
        mesh=mesh,
        in_specs=placed,
        out_specs=(P(None, "gx", "gy", "gz"), P("gz", "gx", "gy", None)),
        check_vma=False,
    )
```

```python
import jax
import jax.numpy as jnp
from jax import lax
from jax.experimental import pallas as pl
from jax.experimental.pallas import tpu as pltpu
from jax.sharding import PartitionSpec as P

COEFFS = (0.8, -0.2, 4.0 / 105.0, -1.0 / 280.0)
TIME_STEP = 0.45
MESH = pl.DeviceIdType.MESH
f32, bf16 = jnp.float32, jnp.bfloat16
NN = (((1,), (0,)), ((), ()))
NT = (((1,), (1,)), ((), ()))
TN = (((0,), (0,)), ((), ()))


def dot(a, b, dims=NN):
    return lax.dot_general(a, b, dims, preferred_element_type=f32)


def split(a):
    high = a.astype(bf16)
    return high, (a - high.astype(f32)).astype(bf16)


def iota(shape, dim):
    return lax.broadcasted_iota(jnp.int32, shape, dim)


def onehot(mask):
    return jnp.where(mask, 1.0, 0.0).astype(bf16)


def stencil(offset):
    value = jnp.zeros(offset.shape, f32)
    for k, c in enumerate(COEFFS):
        value = jnp.where(offset == k + 1, c, value)
        value = jnp.where(offset == -k - 1, -c, value)
    return value


def quadrants(t):
    m, n = t.shape[0] // 2, t.shape[1] // 2
    return t[:m, :n] + (t[m:, :n] + t[:m, n:])


def halves(t):
    n = t.shape[1] // 2
    return t[:, :n] + t[:, n:]


def both(a):
    return jnp.concatenate(split(a), axis=1)


def kernel(
    f_hbm, speeds_hbm, kin_hbm, rank_hbm, xf_hbm, yf_hbm, zf_hbm,
    next_ref, core_ref,
    FX, SX, YB, ZS, ZB, FN, PB, BR, QB, CT, RB, EU, FU, SB, GB, XR, XG, YT, YG, ZT, XF, YF, KIN, SPD, RANK,
    A2, D2, E2, SEL, Z2, X2, W2, SXR, SZR,
    load_sem, small_sem, out_sem, own_sem, ysend, yrecv, zsend, zrecv, z0send, z0recv, xsend, xrecv,
    bsend, brecv, csend, crecv, esend, erecv, fsend, frecv, gsend, grecv,
    xrs, xrr, yrs, yrr, gx_round, z_round,
):
    g, l, q = lax.axis_index("gx"), lax.axis_index("gy"), lax.axis_index("gz")
    h, k = q // 2, lax.rem(q, 2)
    ring = h * 8 + l
    partner = q + 1 - 2 * k

    def ring_device(r):
        return (g, lax.rem(r, 8), 2 * (r // 8) + k)

    def remote(src, dst, send, recv, device):
        return pltpu.make_async_remote_copy(
            src_ref=src, dst_ref=dst, send_sem=send, recv_sem=recv,
            device_id=device, device_id_type=MESH)

    def load(x):
        return pltpu.make_async_copy(f_hbm.at[:, x], FX.at[4 + x], load_sem.at[x])

    def ycopy(s, d, p):
        X = (FX, SX)[s]
        rows = pl.ds(4 * d, 4)
        return remote(X.at[4 + p, :, rows], YB.at[s, p, :, rows], ysend.at[s, d, p],
                      yrecv.at[s, d, p], (g, l + 2 * d - 1, q))

    def z0copy(d):
        rows = pl.ds(4 * d, 4)
        return remote(ZS.at[0, :, rows], ZB.at[0, :, rows], z0send.at[d], z0recv.at[d],
                      (g, l, q + 2 * d - 1))

    def zcopy(d, p):
        rows = pl.ds(4 * d, 4)
        return remote(ZS.at[1, p, rows], ZB.at[1, p, rows], zsend.at[d, p], zrecv.at[d, p],
                      (g, l, q + 2 * d - 1))

    def xcopy(s, d, i):
        X = (FX, SX)[s]
        src, dst = (12 + i, i) if d else (4 + i, 16 + i)
        return remote(X.at[src], X.at[dst], xsend.at[s, d, i], xrecv.at[s, d, i],
                      (g + 2 * d - 1, l, q))

    def bcopy(x):
        return remote(PB.at[1 - k, x], BR.at[x], bsend.at[x], brecv.at[x], (g, l, partner))

    def can_send(index, last, d):
        return index < last if d else index > 0

    def can_recv(index, last, d):
        return index > 0 if d else index < last

    barrier = pltpu.get_barrier_semaphore()

    def greet(device):
        pl.semaphore_signal(barrier, inc=1, device_id=device, device_id_type=MESH)

    def gx_device(i):
        return (lax.rem(g + i, 16), l, q)

    far = jnp.logical_or(q == 1, q == 2)
    for i in (1, 15):
        greet(gx_device(i))
        greet(ring_device(lax.rem(ring + i, 16)))
    greet((g, l, partner))

    @pl.when(far)
    def _():
        greet((g, l, 3 - q))

    for x in range(12):
        load(x).start()
    small = [
        pltpu.make_async_copy(src, dst, small_sem.at[i])
        for i, (src, dst) in enumerate((
            (speeds_hbm, SPD), (kin_hbm, KIN), (rank_hbm, RANK), (xf_hbm, XF),
            (yf_hbm, YF), (zf_hbm, ZT.at[pl.ds(0, 54)]),
        ))
    ]
    YT[...] = jnp.zeros((8, 128), f32)
    ZT[...] = jnp.zeros((64, 128), f32)
    for copy in small:
        copy.start()

    def tell(n):
        for i in (1 << n, 16 - (1 << n)):
            pl.semaphore_signal(gx_round.at[n], inc=1, device_id=gx_device(i), device_id_type=MESH)
            pl.semaphore_signal(z_round.at[n], inc=1, device_id=ring_device(lax.rem(ring + i, 16)),
                                device_id_type=MESH)

    def hear(n):
        pl.semaphore_wait(gx_round.at[n], 2)
        pl.semaphore_wait(z_round.at[n], 2)

    for d in range(2):
        rows = pl.ds(4 * d, 4)

        @pl.when(jnp.logical_not(can_recv(l, 7, d)))
        def _():
            YB[:, :, :, rows, :] = jnp.zeros((2, 12, 16, 4, 128), f32)

        @pl.when(jnp.logical_not(can_recv(q, 3, d)))
        def _():
            ZB[:, :, rows, :] = jnp.zeros((2, 12, 4, 128), f32)

        @pl.when(jnp.logical_not(can_recv(g, 15, d)))
        def _():
            for X in (FX, SX):
                X[pl.ds(0 if d else 16, 4)] = jnp.zeros((4, 16, 8, 128), f32)

    i8, c8 = iota((8, 256), 0), jnp.bitwise_and(iota((8, 256), 1), 127)
    SEL[...] = onehot(c8 == jnp.where(i8 < 4, i8, 120 + i8))
    for x in range(12):
        load(x).wait()

    def first_z(x, c):
        ZS[0, x] = dot(SEL[...], both(FX[4 + x].reshape(128, 128)), NT)
        return c

    lax.fori_loop(0, 12, first_z, 0)
    pl.semaphore_wait(barrier, 5 + jnp.where(far, 1, 0))
    for d in range(2):
        pl.when(can_send(q, 3, d))(lambda: z0copy(d).start())

    def send_edges(j, c):
        for p in (5 - j, 6 + j):
            for d in range(2):
                pl.when(can_send(l, 7, d))(lambda: ycopy(0, d, p).start())
        return c

    def send_planes(i, c):
        pl.when(can_send(g, 15, 1))(lambda: xcopy(0, 1, 3 - i).start())
        pl.when(can_send(g, 15, 0))(lambda: xcopy(0, 0, i).start())
        return c

    lax.fori_loop(0, 2, send_edges, 0)
    lax.fori_loop(0, 4, send_planes, 0)
    lax.fori_loop(2, 6, send_edges, 0)
    tell(0)
    for copy in small:
        copy.wait()

    row, col = iota((128, 256), 0), iota((128, 256), 1)
    v, y = row >> 3, jnp.bitwise_and(row, 7)
    own = col < 128
    cc = jnp.bitwise_and(col, 127)
    w, s8 = cc >> 3, jnp.bitwise_and(cc, 7)
    y2 = jnp.where(own, s8, jnp.where(s8 < 4, 8 + s8, s8 - 8))
    rows_v = onehot(iota((128, 16), 0) >> 3 == iota((128, 16), 1))
    cols_w = onehot(jnp.bitwise_and(iota((16, 256), 1), 127) >> 3 == iota((16, 256), 0))

    def spread(value):
        total = jnp.zeros((128, 256), f32)
        for part in split(value):
            total = total + dot(dot(rows_v, part).astype(bf16), cols_w)
        return total

    lane = iota((16, 16), 1) == iota((16, 16), 0)

    def speed_rows(d):
        total = jnp.zeros((128, 256), f32)
        for part in split(jnp.where(lane, SPD[d : d + 1, :], 0.0)):
            total = total + dot(rows_v, dot(part, jnp.ones((16, 256), bf16)).astype(bf16))
        return -TIME_STEP * total

    SXR[...] = speed_rows(0)[:, :128]
    SZR[...] = speed_rows(2)[:, :128]
    A = jnp.where(y == y2, TIME_STEP * spread(KIN[...]), 0.0)
    A = A + jnp.where(v == w, speed_rows(1) * stencil(y2 - y), 0.0)
    A2[...] = jnp.concatenate(split(A), axis=0)
    D = both(stencil(iota((128, 128), 0) - iota((128, 128), 1)))
    D2[...] = jnp.concatenate([D, D], axis=0)
    i8, z8 = iota((8, 128), 0), iota((8, 128), 1)
    E = both(stencil(jnp.where(i8 < 4, 128 + i8, i8 - 8) - z8))
    E2[...] = jnp.concatenate([E, E], axis=0)
    Z = ZT[...]
    none = jnp.zeros((64, 128), f32)
    Z = jnp.concatenate([jnp.concatenate([Z, none], axis=1), jnp.concatenate([none, Z], axis=1)], axis=0)
    Z2[...] = jnp.concatenate(split(Z), axis=0)

    XR[...] = jnp.zeros((16, 128), f32)
    for i in range(12):
        XR[i : i + 1, 0:96] = XF[pl.ds(RANK[6 + i // 2 if i % 2 else 5 - i // 2], 1), :]
    YT[:, 0:64] = YF[...]
    XG[g] = XR[...]
    YG[l] = YT[...]

    def xrow(peer, slot):
        return remote(XR, XG.at[slot], xrs.at[peer], xrr.at[slot], (peer, l, q))

    def yrow(peer, slot):
        return remote(YT, YG.at[slot], yrs.at[peer], yrr.at[slot], (g, peer, q))

    def over(n, me, act):
        def body(i, c):
            act(lax.rem(me + i, n))
            return c
        lax.fori_loop(1, n, body, 0)

    hear(0)
    tell(1)

    def change(X, s, p):
        center = X[4 + p].reshape(128, 128)
        F = jnp.concatenate([both(center), both(YB[s, p].reshape(128, 128))], axis=0)
        t = dot(A2[...], F)
        zt = dot(F[:128], D2[...])
        zt = zt + dot(jnp.concatenate(split(ZB[s, p]), axis=0), E2[...], TN)
        xt = jnp.zeros((16, 8, 128), f32)
        for i, c in enumerate(COEFFS):
            xt = xt + c * (X[5 + i + p] - X[3 - i + p])
        return center, quadrants(t) + SZR[...] * halves(zt) + SXR[...] * xt.reshape(128, 128)

    def wait_halo(j, s):
        for p in (5 - j, 6 + j):
            for d in range(2):
                pl.when(can_recv(l, 7, d))(lambda: ycopy(s, d, p).wait_recv())
                if s:
                    pl.when(can_recv(q, 3, d))(lambda: zcopy(d, p).wait_recv())
        for d in range(2):
            i = 5 - j if d else j - 2
            pl.when(jnp.logical_and(j >= 2, can_recv(g, 15, d)))(
                lambda: xcopy(s, d, i).wait_recv())

    for d in range(2):
        pl.when(can_recv(q, 3, d))(lambda: z0copy(d).wait_recv())

    def first(j, c):
        @pl.when(j == 2)
        def _():
            hear(1)
            tell(2)

        wait_halo(j, 0)
        for p in (5 - j, 6 + j):
            center, add = change(FX, 0, p)
            section = center + add
            SX[4 + p] = section.reshape(16, 8, 128)
            ZS[1, p] = dot(SEL[...], both(section), NT)
            for d in range(2):
                pl.when(can_send(q, 3, d))(lambda: zcopy(d, p).start())
                pl.when(can_send(l, 7, d))(lambda: ycopy(1, d, p).start())
        for d in range(2):
            i = j - 2 if d else 5 - j
            pl.when(jnp.logical_and(j >= 2, can_send(g, 15, d)))(
                lambda: xcopy(1, d, i).start())
        return c

    lax.fori_loop(0, 6, first, 0)

    hear(2)
    over(16, g, lambda peer: xrow(peer, g).start())
    over(8, l, lambda peer: yrow(peer, l).start())

    def projections():
        over(16, g, lambda peer: xrow(peer, peer).wait_recv())
        over(8, l, lambda peer: yrow(peer, peer).wait_recv())
        shape = (4, 12, 8, 256)
        src = 4 * iota(shape, 0) + (iota(shape, 2) >> 1)
        pick = onehot((16 * src + iota(shape, 1) == iota(shape, 3)).reshape(384, 256))
        shape = (6, 4, 8, 128)
        rank = 24 * iota(shape, 1) + 6 * (iota(shape, 2) >> 1) + iota(shape, 0)
        ranks = onehot((rank == iota(shape, 3)).reshape(192, 128))
        same = jnp.bitwise_and(iota((192, 384), 0) ^ iota((192, 384), 1), 1) == 0
        for n, part in enumerate(split(XG[...].reshape(256, 128))):
            rows = dot(ranks, dot(pick, part).astype(bf16), NT)
            X2[192 * n : 192 * n + 192, :] = jnp.where(same, rows, 0.0).astype(bf16)
        Y = YG[...].reshape(64, 128)
        Y = Y + pltpu.roll(Y, 64, 1)
        col = iota((64, 256), 1)
        pick = onehot(8 * jnp.bitwise_and(col >> 4, 7) + jnp.bitwise_and(col, 7) == iota((64, 256), 0))
        same = iota((128, 256), 0) >> 6 == jnp.bitwise_and(iota((128, 256), 1) >> 3, 1)
        for n, part in enumerate(split(Y)):
            W2[128 * n : 128 * n + 128, :] = jnp.where(same, dot(part, pick, TN), 0.0).astype(bf16)

    def put(p):
        return pltpu.make_async_copy(FN.at[p], next_ref.at[:, p], out_sem.at[p])

    def place(d):
        return d // 4, pl.ds(2 * lax.rem(d, 4), 2)

    def ccopy(n, peer, slot):
        t, rows = place(peer)
        t2, rows2 = place(slot)
        part = pl.ds(8 * n, 8 - 4 * n)
        return remote(QB.at[part, t, rows], CT.at[t2, part, rows2], csend.at[n, peer],
                      crecv.at[n, slot], (peer, l, q))

    def send_part(n):
        def add_partner(x, c):
            bcopy(x).wait_recv()
            QB[x] = PB[k, x] + BR[x]
            return c

        lax.fori_loop(8 * n, 8 + 4 * n, add_partner, 0)
        over(16, g, lambda peer: ccopy(n, peer, g).start())

    def second(j, c):
        wait_halo(j, 1)
        for i, p in enumerate((5 - j, 6 + j)):
            center, add = change(SX, 1, p)
            new = 0.5 * (FX[4 + p].reshape(128, 128) + center + add)
            FN[p] = new.reshape(16, 8, 128)
            put(p).start()
            new = new.reshape(8, 2, 8, 128)
            pair = jnp.concatenate([new[:, 0].reshape(64, 128), new[:, 1].reshape(64, 128)], axis=1)
            z = quadrants(dot(jnp.concatenate(split(pair), axis=0), Z2[...], NT))
            z = z.reshape(2, 2, 2, 8, 128)
            for n in range(2):
                PB[n, 2 * j + i] = z[:, n].reshape(4, 8, 128)
            bcopy(2 * j + i).start()
        return c

    lax.fori_loop(0, 4, second, 0)
    projections()
    second(4, 0)
    send_part(0)
    second(5, 0)

    send_part(1)

    def ecopy(peer, slot):
        t, rows = place(peer)
        t2, rows2 = place(slot)
        return remote(RB.at[:, t, rows], EU.at[t2, :, rows2], esend.at[peer], erecv.at[slot],
                      (peer, l, q))

    t, rows = place(g)
    mine = pltpu.make_async_copy(QB.at[:, t, rows], CT.at[t, :, rows], own_sem.at[0])
    mine.start()
    mine.wait()
    for n in range(2):
        over(16, g, lambda peer: ccopy(n, peer, peer).wait_recv())
    R = quadrants(dot(X2[...], both(CT[...].reshape(384, 128))))
    RB[...] = R.reshape(6, 4, 8, 128)
    over(16, g, lambda peer: ecopy(peer, g).start())
    mine = pltpu.make_async_copy(RB.at[:, t, rows], EU.at[t, :, rows], own_sem.at[1])
    mine.start()
    mine.wait()
    over(16, g, lambda peer: ecopy(peer, peer).wait_recv())

    units = [(u, a, b) for u in range(2) for a in range(3) for b in range(2)]

    def fcopy(unit):
        u, a, b = unit
        return remote(EU.at[2 * b + u, pl.ds(2 * a, 2)], FU.at[ring], fsend.at[8 * b + 3 * u + a],
                      frecv.at[ring], (g, 1 + 3 * u + a, 2 * b + k))

    def fcome(r):
        return remote(EU.at[0, pl.ds(0, 2)], FU.at[r], fsend.at[0], frecv.at[r], ring_device(r))

    def to_self(unit):
        u, a, b = unit
        return jnp.logical_and(l == 1 + 3 * u + a, h == b)

    for unit in units:
        pl.when(jnp.logical_not(to_self(unit)))(lambda: fcopy(unit).start())

        @pl.when(to_self(unit))
        def _():
            u, a, b = unit
            FU[ring] = EU[2 * b + u, pl.ds(2 * a, 2)]

    def gcopy(there, slot):
        return remote(SB.at[:, there], GB.at[slot], gsend.at[there], grecv.at[slot], (g, there, q))

    works = jnp.logical_and(l >= 1, l <= 6)

    @pl.when(works)
    def _():
        over(16, ring, lambda r: fcome(r).wait_recv())
        S = quadrants(dot(W2[...], both(FU[...].reshape(256, 128))))
        SB[...] = S.reshape(2, 8, 8, 128)
        over(8, l, lambda there: gcopy(there, l - 1).start())
        GB[l - 1] = SB[:, l]

    for e in range(6):
        pl.when(l != e + 1)(lambda: gcopy(l, e).wait_recv())
    for u in range(2):
        for a in range(6):
            tile = GB[3 * u + a // 2, a % 2]
            core_ref[2 * u, a] = tile[:, 0:54]
            core_ref[2 * u + 1, a] = pltpu.roll(tile, 64, 1)[:, 0:54]

    def done(p, c):
        for s in range(2):
            for d in range(2):
                pl.when(can_send(l, 7, d))(lambda: ycopy(s, d, p).wait_send())
        for d in range(2):
            pl.when(can_send(q, 3, d))(lambda: zcopy(d, p).wait_send())
        bcopy(p).wait_send()
        put(p).wait()
        return c

    lax.fori_loop(0, 12, done, 0)
    for d in range(2):
        pl.when(can_send(q, 3, d))(lambda: z0copy(d).wait_send())
        for s in range(2):
            for i in range(4):
                pl.when(can_send(g, 15, d))(lambda: xcopy(s, d, i).wait_send())

    def done_peer(peer):
        xrow(peer, g).wait_send()
        for n in range(2):
            ccopy(n, peer, g).wait_send()
        ecopy(peer, g).wait_send()

    over(16, g, done_peer)
    over(8, l, lambda peer: yrow(peer, l).wait_send())
    for unit in units:
        pl.when(jnp.logical_not(to_self(unit)))(lambda: fcopy(unit).wait_send())

    @pl.when(works)
    def _():
        over(8, l, lambda there: gcopy(there, l - 1).wait_send())


def local(fields, speeds, kinetics, block_rank, x_factor, y_factor, z_factor):
    vmem, dma = pltpu.VMEM, pltpu.SemaphoreType.DMA
    in_vmem = pl.BlockSpec(memory_space=pltpu.VMEM)
    in_hbm = pl.BlockSpec(memory_space=pltpu.HBM)
    return pl.pallas_call(
        kernel,
        out_shape=(
            jax.ShapeDtypeStruct(fields.shape, f32),
            jax.ShapeDtypeStruct((4, 6, 8, 54), f32),
        ),
        in_specs=[in_hbm] * 7,
        out_specs=(in_hbm, in_vmem),
        scratch_shapes=[
            vmem((20, 16, 8, 128), f32),
            vmem((20, 16, 8, 128), f32),
            vmem((2, 12, 16, 8, 128), f32),
            vmem((2, 12, 8, 128), f32),
            vmem((2, 12, 8, 128), f32),
            vmem((12, 16, 8, 128), f32),
            vmem((2, 12, 4, 8, 128), f32),
            vmem((12, 4, 8, 128), f32),
            vmem((12, 4, 8, 128), f32),
            vmem((4, 12, 8, 128), f32),
            vmem((6, 4, 8, 128), f32),
            vmem((4, 6, 8, 128), f32),
            vmem((16, 2, 8, 128), f32),
            vmem((2, 8, 8, 128), f32),
            vmem((6, 2, 8, 128), f32),
            vmem((16, 128), f32),
            vmem((16, 16, 128), f32),
            vmem((8, 128), f32),
            vmem((8, 8, 128), f32),
            vmem((64, 128), f32),
            vmem((192, 96), f32),
            vmem((8, 64), f32),
            vmem((16, 16), f32),
            vmem((3, 16), f32),
            pltpu.SMEM((12,), jnp.int32),
            vmem((256, 256), bf16),
            vmem((256, 256), bf16),
            vmem((16, 256), bf16),
            vmem((8, 256), bf16),
            vmem((256, 256), bf16),
            vmem((384, 384), bf16),
            vmem((256, 256), bf16),
            vmem((128, 128), f32),
            vmem((128, 128), f32),
            dma((12,)), dma((6,)), dma((12,)), dma((2,)),
            dma((2, 2, 12)), dma((2, 2, 12)),
            dma((2, 12)), dma((2, 12)), dma((2,)), dma((2,)),
            dma((2, 2, 4)), dma((2, 2, 4)),
            dma((12,)), dma((12,)),
            dma((2, 16)), dma((2, 16)), dma((16,)), dma((16,)), dma((16,)), dma((16,)),
            dma((8,)), dma((8,)),
            dma((16,)), dma((16,)), dma((8,)), dma((8,)),
            pltpu.SemaphoreType.REGULAR((3,)), pltpu.SemaphoreType.REGULAR((3,)),
        ],
        compiler_params=pltpu.CompilerParams(
            collective_id=0, has_side_effects=True, vmem_limit_bytes=60 * 1024 * 1024),
    )(fields, speeds, kinetics, block_rank, x_factor, y_factor, z_factor.T)


def solution(mesh):
    placed = (P(None, "gx", "gy", "gz"), P(), P(), P("gx"), P(), P("gy", None), P("gz", None))
    return jax.shard_map(
        local,
        mesh=mesh,
        in_specs=placed,
        out_specs=(P(None, "gx", "gy", "gz"), P("gz", "gx", "gy", None)),
        check_vma=False,
    )
```

```python
import jax
import jax.numpy as jnp
from jax import lax
from jax.experimental import pallas as pl
from jax.experimental.pallas import tpu as pltpu
from jax.sharding import PartitionSpec as P

COEFFS = (0.8, -0.2, 4.0 / 105.0, -1.0 / 280.0)
TIME_STEP = 0.45
MESH = pl.DeviceIdType.MESH
f32, bf16 = jnp.float32, jnp.bfloat16
NN = (((1,), (0,)), ((), ()))
NT = (((1,), (1,)), ((), ()))
TN = (((0,), (0,)), ((), ()))


def dot(a, b, dims=NN):
    return lax.dot_general(a, b, dims, preferred_element_type=f32)


def split(a):
    high = a.astype(bf16)
    return high, (a - high.astype(f32)).astype(bf16)


def iota(shape, dim):
    return lax.broadcasted_iota(jnp.int32, shape, dim)


def onehot(mask):
    return jnp.where(mask, 1.0, 0.0).astype(bf16)


def stencil(offset):
    value = jnp.zeros(offset.shape, f32)
    for k, c in enumerate(COEFFS):
        value = jnp.where(offset == k + 1, c, value)
        value = jnp.where(offset == -k - 1, -c, value)
    return value


def quadrants(t):
    m, n = t.shape[0] // 2, t.shape[1] // 2
    return t[:m, :n] + (t[m:, :n] + t[:m, n:])


def halves(t):
    n = t.shape[1] // 2
    return t[:, :n] + t[:, n:]


def both(a):
    return jnp.concatenate(split(a), axis=1)


def stacked(a):
    return jnp.concatenate(split(a), axis=0)


def product(a, b):
    return quadrants(dot(stacked(a), both(b)))


def paired(a):
    a = a.reshape(8, 2, 8, 128)
    return jnp.concatenate([a[:, 0].reshape(64, 128), a[:, 1].reshape(64, 128)], axis=1)


def kernel(
    f_hbm, speeds_hbm, kin_hbm, rank_hbm, xf_hbm, yf_hbm, zf_hbm,
    next_ref, core_ref,
    FX, SX, YB, ZS, ZB, FN, PB, BR, QB, CT, RB, EU, FU, SB, GB, XR, XG, YT, YG, ZT, ZE, ZX, XF, YF, KIN, SPD, RANK,
    A2, K2, D2, E2, SEL, Z2, X2, W2, SXR, SZR,
    load_sem, small_sem, out_sem, own_sem, ysend, yrecv, zsend, zrecv, z0send, z0recv, zfsend, zfrecv, xsend, xrecv,
    bsend, brecv, csend, crecv, esend, erecv, fsend, frecv, gsend, grecv,
    xrs, xrr, yrs, yrr, gx_round, z_round,
):
    g, l, q = lax.axis_index("gx"), lax.axis_index("gy"), lax.axis_index("gz")
    h, k = q // 2, lax.rem(q, 2)
    ring = h * 8 + l
    partner = q + 1 - 2 * k

    def ring_device(r):
        return (g, lax.rem(r, 8), 2 * (r // 8) + k)

    def remote(src, dst, send, recv, device):
        return pltpu.make_async_remote_copy(
            src_ref=src, dst_ref=dst, send_sem=send, recv_sem=recv,
            device_id=device, device_id_type=MESH)

    def load(x):
        return pltpu.make_async_copy(f_hbm.at[:, x], FX.at[4 + x], load_sem.at[x])

    def ycopy(s, d, p):
        X = (FX, SX)[s]
        rows = pl.ds(4 * d, 4)
        return remote(X.at[4 + p, :, rows], YB.at[s, p, :, rows], ysend.at[s, d, p],
                      yrecv.at[s, d, p], (g, l + 2 * d - 1, q))

    def z0copy(d):
        rows = pl.ds(4 * d, 4)
        return remote(ZS.at[0, :, rows], ZB.at[0, :, rows], z0send.at[d], z0recv.at[d],
                      (g, l, q + 2 * d - 1))

    def zfcopy(d):
        return remote(ZE.at[pl.ds(4 * d, 4)], ZX.at[pl.ds(128 + 4 * d, 4)], zfsend.at[d], zfrecv.at[d],
                      (g, l, q + 2 * d - 1))

    def zcopy(d, p):
        rows = pl.ds(4 * d, 4)
        return remote(ZS.at[1, p, rows], ZB.at[1, p, rows], zsend.at[d, p], zrecv.at[d, p],
                      (g, l, q + 2 * d - 1))

    def xcopy(s, d, i):
        X = (FX, SX)[s]
        src, dst = (12 + i, i) if d else (4 + i, 16 + i)
        return remote(X.at[src], X.at[dst], xsend.at[s, d, i], xrecv.at[s, d, i],
                      (g + 2 * d - 1, l, q))

    def bcopy(x):
        return remote(PB.at[1 - k, x], BR.at[x], bsend.at[x], brecv.at[x], (g, l, partner))

    def can_send(index, last, d):
        return index < last if d else index > 0

    def can_recv(index, last, d):
        return index > 0 if d else index < last

    barrier = pltpu.get_barrier_semaphore()

    def greet(device):
        pl.semaphore_signal(barrier, inc=1, device_id=device, device_id_type=MESH)

    def gx_device(i):
        return (lax.rem(g + i, 16), l, q)

    far = jnp.logical_or(q == 1, q == 2)
    for i in (1, 15):
        greet(gx_device(i))
        greet(ring_device(lax.rem(ring + i, 16)))
    greet((g, l, partner))

    @pl.when(far)
    def _():
        greet((g, l, 3 - q))

    for x in range(12):
        load(x).start()
    small = [
        pltpu.make_async_copy(src, dst, small_sem.at[i])
        for i, (src, dst) in enumerate((
            (speeds_hbm, SPD), (kin_hbm, KIN), (rank_hbm, RANK), (xf_hbm, XF),
            (yf_hbm, YF), (zf_hbm, ZT.at[pl.ds(0, 54)]),
        ))
    ]
    YT[...] = jnp.zeros((8, 128), f32)
    ZT[...] = jnp.zeros((128, 128), f32)
    ZX[pl.ds(136, 120)] = jnp.zeros((120, 128), f32)
    for copy in small:
        copy.start()

    def tell(n):
        for i in (1 << n, 16 - (1 << n)):
            pl.semaphore_signal(gx_round.at[n], inc=1, device_id=gx_device(i), device_id_type=MESH)
            pl.semaphore_signal(z_round.at[n], inc=1, device_id=ring_device(lax.rem(ring + i, 16)),
                                device_id_type=MESH)

    def hear(n):
        pl.semaphore_wait(gx_round.at[n], 2)
        pl.semaphore_wait(z_round.at[n], 2)

    for d in range(2):
        rows = pl.ds(4 * d, 4)

        @pl.when(jnp.logical_not(can_recv(l, 7, d)))
        def _():
            YB[:, :, :, rows, :] = jnp.zeros((2, 12, 16, 4, 128), f32)

        @pl.when(jnp.logical_not(can_recv(q, 3, d)))
        def _():
            ZB[:, :, rows, :] = jnp.zeros((2, 12, 4, 128), f32)
            ZX[pl.ds(128 + 4 * d, 4)] = jnp.zeros((4, 128), f32)

        @pl.when(jnp.logical_not(can_recv(g, 15, d)))
        def _():
            for X in (FX, SX):
                X[pl.ds(0 if d else 16, 4)] = jnp.zeros((4, 16, 8, 128), f32)

    i8, c8 = iota((8, 256), 0), jnp.bitwise_and(iota((8, 256), 1), 127)
    SEL[...] = onehot(c8 == jnp.where(i8 < 4, i8, 120 + i8))
    for x in range(12):
        load(x).wait()

    def first_z(x, c):
        ZS[0, x] = dot(SEL[...], both(FX[4 + x].reshape(128, 128)), NT)
        return c

    lax.fori_loop(0, 12, first_z, 0)
    for copy in small:
        copy.wait()
    ZX[pl.ds(0, 128)] = ZT[...].T
    ZE[pl.ds(0, 4)] = ZX[pl.ds(0, 4)]
    ZE[pl.ds(4, 4)] = ZX[pl.ds(124, 4)]
    pl.semaphore_wait(barrier, 5 + jnp.where(far, 1, 0))
    for d in range(2):
        pl.when(can_send(q, 3, d))(lambda: z0copy(d).start())
        pl.when(can_send(q, 3, d))(lambda: zfcopy(d).start())

    def send_edges(j, c):
        for p in (5 - j, 6 + j):
            for d in range(2):
                pl.when(can_send(l, 7, d))(lambda: ycopy(0, d, p).start())
        return c

    def send_planes(i, c):
        pl.when(can_send(g, 15, 1))(lambda: xcopy(0, 1, 3 - i).start())
        pl.when(can_send(g, 15, 0))(lambda: xcopy(0, 0, i).start())
        return c

    lax.fori_loop(0, 2, send_edges, 0)
    lax.fori_loop(0, 4, send_planes, 0)
    lax.fori_loop(2, 6, send_edges, 0)
    tell(0)

    row, col = iota((128, 256), 0), iota((128, 256), 1)
    v, y = row >> 3, jnp.bitwise_and(row, 7)
    own = col < 128
    cc = jnp.bitwise_and(col, 127)
    w, s8 = cc >> 3, jnp.bitwise_and(cc, 7)
    y2 = jnp.where(own, s8, jnp.where(s8 < 4, 8 + s8, s8 - 8))
    rows_v = onehot(iota((128, 16), 0) >> 3 == iota((128, 16), 1))
    cols_w = onehot(jnp.bitwise_and(iota((16, 256), 1), 127) >> 3 == iota((16, 256), 0))

    def spread(value):
        total = jnp.zeros((128, 256), f32)
        for part in split(value):
            total = total + dot(dot(rows_v, part).astype(bf16), cols_w)
        return total

    lane = iota((16, 16), 1) == iota((16, 16), 0)

    def speed_rows(d):
        total = jnp.zeros((128, 256), f32)
        for part in split(jnp.where(lane, SPD[d : d + 1, :], 0.0)):
            total = total + dot(rows_v, dot(part, jnp.ones((16, 256), bf16)).astype(bf16))
        return -TIME_STEP * total

    SXR[...] = speed_rows(0)[:, :128]
    SZR[...] = speed_rows(2)[:, :128]
    A = jnp.where(y == y2, TIME_STEP * spread(KIN[...]), 0.0)
    K2[...] = stacked(A[:, :128])
    A = A + jnp.where(v == w, speed_rows(1) * stencil(y2 - y), 0.0)
    A2[...] = jnp.concatenate(split(A), axis=0)
    D = both(stencil(iota((128, 128), 0) - iota((128, 128), 1)))
    D2[...] = jnp.concatenate([D, D], axis=0)
    i8, z8 = iota((8, 128), 0), iota((8, 128), 1)
    E = both(stencil(jnp.where(i8 < 4, 128 + i8, i8 - 8) - z8))
    E2[...] = jnp.concatenate([E, E], axis=0)
    XR[...] = jnp.zeros((16, 128), f32)
    for i in range(12):
        XR[i : i + 1, 0:96] = XF[pl.ds(RANK[6 + i // 2 if i % 2 else 5 - i // 2], 1), :]
    YT[:, 0:64] = YF[...]
    XG[g] = XR[...]
    YG[l] = YT[...]

    def xrow(peer, slot):
        return remote(XR, XG.at[slot], xrs.at[peer], xrr.at[slot], (peer, l, q))

    def yrow(peer, slot):
        return remote(YT, YG.at[slot], yrs.at[peer], yrr.at[slot], (g, peer, q))

    def over(n, me, act):
        def body(i, c):
            act(lax.rem(me + i, n))
            return c
        lax.fori_loop(1, n, body, 0)

    hear(0)
    tell(1)
    hear(1)
    tell(2)

    def change(X, s, p):
        center = X[4 + p].reshape(128, 128)
        F = jnp.concatenate([both(center), both(YB[s, p].reshape(128, 128))], axis=0)
        t = dot(A2[...], F)
        zt = dot(F[:128], D2[...])
        zt = zt + dot(jnp.concatenate(split(ZB[s, p]), axis=0), E2[...], TN)
        xt = jnp.zeros((16, 8, 128), f32)
        for i, c in enumerate(COEFFS):
            xt = xt + c * (X[5 + i + p] - X[3 - i + p])
        return center, quadrants(t) + SZR[...] * halves(zt) + SXR[...] * xt.reshape(128, 128)

    def wait_halo(j, s):
        for p in (5 - j, 6 + j):
            for d in range(2):
                pl.when(can_recv(l, 7, d))(lambda: ycopy(s, d, p).wait_recv())
                if s:
                    pl.when(can_recv(q, 3, d))(lambda: zcopy(d, p).wait_recv())
        for d in range(2):
            i = 5 - j if d else j - 2
            pl.when(jnp.logical_and(j >= 2, can_recv(g, 15, d)))(
                lambda: xcopy(s, d, i).wait_recv())

    for d in range(2):
        pl.when(can_recv(q, 3, d))(lambda: z0copy(d).wait_recv())
        pl.when(can_recv(q, 3, d))(lambda: zfcopy(d).wait_recv())

    row, col = iota((128, 256), 0), iota((128, 256), 1)
    Z = ZX[pl.ds(0, 128)]
    DZ = product(stencil(row - jnp.where(col < 132, col, col - 136)), ZX[...])
    for n, a in enumerate((Z, DZ)):
        Z2[256 * n : 256 * n + 256, :] = both(jnp.concatenate([a, pltpu.roll(a, 64, 1)], axis=0))

    def first(j, c):
        @pl.when(j == 4)
        def _():
            hear(2)
            over(16, g, lambda peer: xrow(peer, g).start())
            over(8, l, lambda peer: yrow(peer, l).start())

        wait_halo(j, 0)
        for i, p in enumerate((5 - j, 6 + j)):
            center, add = change(FX, 0, p)
            section = center + add
            SX[4 + p] = section.reshape(16, 8, 128)
            parts = both(section)
            ZS[1, p] = dot(SEL[...], parts, NT)
            mixed = 0.5 * (FX[4 + p].reshape(128, 128) + section + quadrants(dot(K2[...], parts)))
            both_z = jnp.concatenate([paired(mixed), paired(0.5 * SZR[...] * section)], axis=1)
            z0 = quadrants(dot(stacked(both_z), Z2[...])).reshape(2, 2, 2, 8, 128)
            z1 = quadrants(dot(stacked(paired(section)), Z2[0:256, :])).reshape(2, 2, 2, 8, 128)
            for n in range(2):
                PB[n, 2 * j + i, 0] = z0[:, n].reshape(4, 8, 128)
                PB[n, 2 * j + i, 1] = z1[:, n].reshape(4, 8, 128)
            bcopy(2 * j + i).start()
            for d in range(2):
                pl.when(can_send(q, 3, d))(lambda: zcopy(d, p).start())
                pl.when(can_send(l, 7, d))(lambda: ycopy(1, d, p).start())
        return c

    def projections():
        over(16, g, lambda peer: xrow(peer, peer).wait_recv())
        over(8, l, lambda peer: yrow(peer, peer).wait_recv())
        shape = (4, 12, 8, 256)
        src = 4 * iota(shape, 0) + (iota(shape, 2) >> 1)
        pick = onehot((16 * src + iota(shape, 1) == iota(shape, 3)).reshape(384, 256))
        shape = (6, 4, 8, 128)
        rank = 24 * iota(shape, 1) + 6 * (iota(shape, 2) >> 1) + iota(shape, 0)
        ranks = onehot((rank == iota(shape, 3)).reshape(192, 128))
        same = jnp.bitwise_and(iota((192, 384), 0) ^ iota((192, 384), 1), 1) == 0
        def plane(index):
            step, n = jnp.bitwise_and(index, 15) >> 1, jnp.bitwise_and(index, 1)
            return 12 * (index >> 4) + jnp.where(n == 1, 6 + step, 5 - step)

        X = XG[...].reshape(256, 128)
        DX = product(stencil(plane(iota((256, 256), 0)) - plane(iota((256, 256), 1))), X)
        for m, a in enumerate((X, DX)):
            for n, part in enumerate(split(a)):
                rows = dot(ranks, dot(pick, part).astype(bf16), NT)
                X2[192 * n : 192 * n + 192, 384 * m : 384 * m + 384] = jnp.where(same, rows, 0.0).astype(bf16)
        Y = YG[...].reshape(64, 128)
        Y = Y + pltpu.roll(Y, 64, 1)
        DY = product(stencil(iota((64, 64), 0) - iota((64, 64), 1)), Y)
        col = iota((64, 256), 1)
        pick = onehot(8 * jnp.bitwise_and(col >> 4, 7) + jnp.bitwise_and(col, 7) == iota((64, 256), 0))
        same = iota((128, 256), 0) >> 6 == jnp.bitwise_and(iota((128, 256), 1) >> 3, 1)
        for m, a in enumerate((Y, DY)):
            for n, part in enumerate(split(a)):
                W2[128 * n : 128 * n + 128, 256 * m : 256 * m + 256] = (
                    jnp.where(same, dot(part, pick, TN), 0.0).astype(bf16))

    def put(p):
        return pltpu.make_async_copy(FN.at[p], next_ref.at[:, p], out_sem.at[p])

    def place(d):
        return d // 4, pl.ds(2 * lax.rem(d, 4), 2)

    def ccopy(n, peer, slot):
        t, rows = place(peer)
        t2, rows2 = place(slot)
        part = pl.ds(8 * n, 8 - 4 * n)
        return remote(QB.at[part, :, t, rows], CT.at[t2, part, :, rows2], csend.at[n, peer],
                      crecv.at[n, slot], (peer, l, q))

    def send_part(n):
        def add_partner(x, c):
            bcopy(x).wait_recv()
            QB[x] = PB[k, x] + BR[x]
            return c

        lax.fori_loop(8 * n, 8 + 4 * n, add_partner, 0)
        over(16, g, lambda peer: ccopy(n, peer, g).start())

    def second(j, c):
        wait_halo(j, 1)
        for p in (5 - j, 6 + j):
            center, add = change(SX, 1, p)
            new = 0.5 * (FX[4 + p].reshape(128, 128) + center + add)
            FN[p] = new.reshape(16, 8, 128)
            put(p).start()
        return c

    lax.fori_loop(0, 5, first, 0)
    send_part(0)
    first(5, 0)

    send_part(1)
    projections()

    def ecopy(peer, slot):
        t, rows = place(peer)
        t2, rows2 = place(slot)
        return remote(RB.at[:, :, t, rows], EU.at[:, t2, :, rows2], esend.at[peer], erecv.at[slot],
                      (peer, l, q))

    t, rows = place(g)
    mine = pltpu.make_async_copy(QB.at[:, :, t, rows], CT.at[t, :, :, rows], own_sem.at[0])
    mine.start()
    mine.wait()
    for n in range(2):
        over(16, g, lambda peer: ccopy(n, peer, peer).wait_recv())
    v0 = 8 * (t // 2) + 4 * k + 2 * lax.rem(t, 2)

    def lane_speeds(d):
        which = iota((1, 16), 1)
        pair = [jnp.sum(jnp.where(which == v0 + n, SPD[d : d + 1, :], 0.0), axis=1, keepdims=True)
                for n in range(2)]
        return -0.5 * TIME_STEP * jnp.where(iota((1, 128), 1) < 64, pair[0], pair[1])

    T0, T1 = CT[:, :, 0].reshape(384, 128), CT[:, :, 1].reshape(384, 128)
    R0 = quadrants(dot(X2[...], both(jnp.concatenate([T0, lane_speeds(0) * T1], axis=0))))
    R1 = quadrants(dot(X2[:, 0:384], both(lane_speeds(1) * T1)))
    RB[0] = R0.reshape(6, 4, 8, 128)
    RB[1] = R1.reshape(6, 4, 8, 128)
    over(16, g, lambda peer: ecopy(peer, g).start())

    def send_sections(i, c):
        pl.when(can_send(g, 15, 1))(lambda: xcopy(1, 1, 3 - i).start())
        pl.when(can_send(g, 15, 0))(lambda: xcopy(1, 0, i).start())
        return c

    lax.fori_loop(0, 4, send_sections, 0)
    mine = pltpu.make_async_copy(RB.at[:, :, t, rows], EU.at[:, t, :, rows], own_sem.at[1])
    mine.start()
    mine.wait()
    lax.fori_loop(0, 2, second, 0)
    over(16, g, lambda peer: ecopy(peer, peer).wait_recv())

    def unit(r):
        n = lax.rem(r, 8) - 1
        return 2 * (r // 8) + n // 3, pl.ds(2 * lax.rem(n, 3), 2)

    def working(r):
        return jnp.logical_and(lax.rem(r, 8) >= 1, lax.rem(r, 8) <= 6)

    def fcopy(r):
        t, ranks = unit(r)
        return remote(EU.at[:, t, ranks], FU.at[ring], fsend.at[r], frecv.at[ring], ring_device(r))

    def fcome(r):
        return remote(EU.at[:, 0, pl.ds(0, 2)], FU.at[r], fsend.at[r], frecv.at[r], ring_device(r))

    def send_unit(i, c):
        r = lax.rem(ring + jnp.where(lax.rem(i, 2) == 0, 8 + i // 2, 7 - i // 2), 16)
        pl.when(working(r))(lambda: fcopy(r).start())
        return c

    lax.fori_loop(0, 15, send_unit, 0)
    works = working(ring)

    @pl.when(works)
    def _():
        t, ranks = unit(ring)
        mine = pltpu.make_async_copy(EU.at[:, t, ranks], FU.at[ring], own_sem.at[0])
        mine.start()
        mine.wait()

    def gcopy(there, slot):
        return remote(SB.at[:, there], GB.at[slot], gsend.at[there], grecv.at[slot], (g, there, q))

    lax.fori_loop(2, 6, second, 0)

    @pl.when(works)
    def _():
        over(16, ring, lambda r: fcome(r).wait_recv())
        U = [FU[:, n].reshape(256, 128) for n in range(2)]
        S = quadrants(dot(W2[...], both(jnp.concatenate(U, axis=0))))
        SB[...] = S.reshape(2, 8, 8, 128)
        over(8, l, lambda there: gcopy(there, l - 1).start())
        GB[l - 1] = SB[:, l]

    def done(p, c):
        for s in range(2):
            for d in range(2):
                pl.when(can_send(l, 7, d))(lambda: ycopy(s, d, p).wait_send())
        for d in range(2):
            pl.when(can_send(q, 3, d))(lambda: zcopy(d, p).wait_send())
        bcopy(p).wait_send()
        put(p).wait()
        return c

    lax.fori_loop(0, 12, done, 0)
    for d in range(2):
        pl.when(can_send(q, 3, d))(lambda: z0copy(d).wait_send())
        pl.when(can_send(q, 3, d))(lambda: zfcopy(d).wait_send())
        for s in range(2):
            for i in range(4):
                pl.when(can_send(g, 15, d))(lambda: xcopy(s, d, i).wait_send())

    def done_peer(peer):
        xrow(peer, g).wait_send()
        for n in range(2):
            ccopy(n, peer, g).wait_send()
        ecopy(peer, g).wait_send()

    over(16, g, done_peer)
    over(8, l, lambda peer: yrow(peer, l).wait_send())
    over(16, ring, lambda r: pl.when(working(r))(lambda: fcopy(r).wait_send()))

    for e in range(6):
        pl.when(l != e + 1)(lambda: gcopy(l, e).wait_recv())
    for u in range(2):
        for a in range(6):
            tile = GB[3 * u + a // 2, a % 2]
            core_ref[2 * u, a] = tile[:, 0:54]
            core_ref[2 * u + 1, a] = pltpu.roll(tile, 64, 1)[:, 0:54]

    @pl.when(works)
    def _():
        over(8, l, lambda there: gcopy(there, l - 1).wait_send())


def local(fields, speeds, kinetics, block_rank, x_factor, y_factor, z_factor):
    vmem, dma = pltpu.VMEM, pltpu.SemaphoreType.DMA
    in_vmem = pl.BlockSpec(memory_space=pltpu.VMEM)
    in_hbm = pl.BlockSpec(memory_space=pltpu.HBM)
    return pl.pallas_call(
        kernel,
        out_shape=(
            jax.ShapeDtypeStruct(fields.shape, f32),
            jax.ShapeDtypeStruct((4, 6, 8, 54), f32),
        ),
        in_specs=[in_hbm] * 7,
        out_specs=(in_hbm, in_vmem),
        scratch_shapes=[
            vmem((20, 16, 8, 128), f32),
            vmem((20, 16, 8, 128), f32),
            vmem((2, 12, 16, 8, 128), f32),
            vmem((2, 12, 8, 128), f32),
            vmem((2, 12, 8, 128), f32),
            vmem((12, 16, 8, 128), f32),
            vmem((2, 12, 2, 4, 8, 128), f32),
            vmem((12, 2, 4, 8, 128), f32),
            vmem((12, 2, 4, 8, 128), f32),
            vmem((4, 12, 2, 8, 128), f32),
            vmem((2, 6, 4, 8, 128), f32),
            vmem((2, 4, 6, 8, 128), f32),
            vmem((16, 2, 2, 8, 128), f32),
            vmem((2, 8, 8, 128), f32),
            vmem((6, 2, 8, 128), f32),
            vmem((16, 128), f32),
            vmem((16, 16, 128), f32),
            vmem((8, 128), f32),
            vmem((8, 8, 128), f32),
            vmem((128, 128), f32),
            vmem((8, 128), f32),
            vmem((256, 128), f32),
            vmem((192, 96), f32),
            vmem((8, 64), f32),
            vmem((16, 16), f32),
            vmem((3, 16), f32),
            pltpu.SMEM((12,), jnp.int32),
            vmem((256, 256), bf16),
            vmem((256, 128), bf16),
            vmem((256, 256), bf16),
            vmem((16, 256), bf16),
            vmem((8, 256), bf16),
            vmem((512, 256), bf16),
            vmem((384, 768), bf16),
            vmem((256, 512), bf16),
            vmem((128, 128), f32),
            vmem((128, 128), f32),
            dma((12,)), dma((6,)), dma((12,)), dma((2,)),
            dma((2, 2, 12)), dma((2, 2, 12)),
            dma((2, 12)), dma((2, 12)), dma((2,)), dma((2,)), dma((2,)), dma((2,)),
            dma((2, 2, 4)), dma((2, 2, 4)),
            dma((12,)), dma((12,)),
            dma((2, 16)), dma((2, 16)), dma((16,)), dma((16,)), dma((16,)), dma((16,)),
            dma((8,)), dma((8,)),
            dma((16,)), dma((16,)), dma((8,)), dma((8,)),
            pltpu.SemaphoreType.REGULAR((3,)), pltpu.SemaphoreType.REGULAR((3,)),
        ],
        compiler_params=pltpu.CompilerParams(
            collective_id=0, has_side_effects=True, vmem_limit_bytes=60 * 1024 * 1024),
    )(fields, speeds, kinetics, block_rank, x_factor, y_factor, z_factor.T)


def solution(mesh):
    placed = (P(None, "gx", "gy", "gz"), P(), P(), P("gx"), P(), P("gy", None), P("gz", None))
    return jax.shard_map(
        local,
        mesh=mesh,
        in_specs=placed,
        out_specs=(P(None, "gx", "gy", "gz"), P("gz", "gx", "gy", None)),
        check_vma=False,
    )
```

```python
import jax
import jax.numpy as jnp
from jax import lax
from jax.experimental import pallas as pl
from jax.experimental.pallas import tpu as pltpu
from jax.sharding import PartitionSpec as P

COEFFS = (0.8, -0.2, 4.0 / 105.0, -1.0 / 280.0)
TIME_STEP = 0.45
MESH = pl.DeviceIdType.MESH
f32, bf16 = jnp.float32, jnp.bfloat16
NN = (((1,), (0,)), ((), ()))
NT = (((1,), (1,)), ((), ()))
TN = (((0,), (0,)), ((), ()))


def dot(a, b, dims=NN):
    return lax.dot_general(a, b, dims, preferred_element_type=f32)


def split(a):
    high = a.astype(bf16)
    return high, (a - high.astype(f32)).astype(bf16)


def iota(shape, dim):
    return lax.broadcasted_iota(jnp.int32, shape, dim)


def onehot(mask):
    return jnp.where(mask, 1.0, 0.0).astype(bf16)


def stencil(offset):
    value = jnp.zeros(offset.shape, f32)
    for k, c in enumerate(COEFFS):
        value = jnp.where(offset == k + 1, c, value)
        value = jnp.where(offset == -k - 1, -c, value)
    return value


def quadrants(t):
    m, n = t.shape[0] // 2, t.shape[1] // 2
    return t[:m, :n] + (t[m:, :n] + t[:m, n:])


def halves(t):
    n = t.shape[1] // 2
    return t[:, :n] + t[:, n:]


def both(a):
    return jnp.concatenate(split(a), axis=1)


def stacked(a):
    return jnp.concatenate(split(a), axis=0)


def product(a, b):
    return quadrants(dot(stacked(a), both(b)))


def paired(a):
    a = a.reshape(8, 2, 8, 128)
    return jnp.concatenate([a[:, 0].reshape(64, 128), a[:, 1].reshape(64, 128)], axis=1)


def kernel(
    f_hbm, speeds_hbm, kin_hbm, rank_hbm, xf_hbm, yf_hbm, zf_hbm,
    next_ref, core_ref,
    FX, SX, YB, ZS, ZB, FN, PB, BR, QB, CT, RB, EU, FU, SB, GB, XR, XG, YT, YG, ZT, ZE, ZX, XF, YF, KIN, SPD, RANK,
    A2, K2, D2, E2, SEL, Z2, X2, W2, SXR, SZR,
    load_sem, small_sem, out_sem, own_sem, ysend, yrecv, zsend, zrecv, z0send, z0recv, zfsend, zfrecv, xsend, xrecv,
    bsend, brecv, csend, crecv, esend, erecv, fsend, frecv, gsend, grecv,
    xrs, xrr, yrs, yrr, gx_round, z_round,
):
    g, l, q = lax.axis_index("gx"), lax.axis_index("gy"), lax.axis_index("gz")
    h, k = q // 2, lax.rem(q, 2)
    ring = h * 8 + l
    partner = q + 1 - 2 * k

    def ring_device(r):
        return (g, lax.rem(r, 8), 2 * (r // 8) + k)

    def remote(src, dst, send, recv, device):
        return pltpu.make_async_remote_copy(
            src_ref=src, dst_ref=dst, send_sem=send, recv_sem=recv,
            device_id=device, device_id_type=MESH)

    def load(x):
        return pltpu.make_async_copy(f_hbm.at[:, x], FX.at[4 + x], load_sem.at[x])

    def ycopy(s, d, p):
        X = (FX, SX)[s]
        rows = pl.ds(4 * d, 4)
        return remote(X.at[4 + p, :, rows], YB.at[s, p, :, rows], ysend.at[s, d, p],
                      yrecv.at[s, d, p], (g, l + 2 * d - 1, q))

    def z0copy(d):
        rows = pl.ds(4 * d, 4)
        return remote(ZS.at[0, :, rows], ZB.at[0, :, rows], z0send.at[d], z0recv.at[d],
                      (g, l, q + 2 * d - 1))

    def zfcopy(d):
        return remote(ZE.at[pl.ds(4 * d, 4)], ZX.at[pl.ds(128 + 4 * d, 4)], zfsend.at[d], zfrecv.at[d],
                      (g, l, q + 2 * d - 1))

    def zcopy(d, j):
        rows, pair = pl.ds(4 * d, 4), pl.ds(2 * j, 2)
        return remote(ZS.at[1, pair, rows], ZB.at[1, pair, rows], zsend.at[d, j], zrecv.at[d, j],
                      (g, l, q + 2 * d - 1))

    def xcopy(s, d, i):
        X = (FX, SX)[s]
        src, dst = (12 + i, i) if d else (4 + i, 16 + i)
        return remote(X.at[src], X.at[dst], xsend.at[s, d, i], xrecv.at[s, d, i],
                      (g + 2 * d - 1, l, q))

    def bcopy(x):
        pair = pl.ds(2 * x, 2)
        return remote(PB.at[1 - k, pair], BR.at[pair], bsend.at[x], brecv.at[x], (g, l, partner))

    def can_send(index, last, d):
        return index < last if d else index > 0

    def can_recv(index, last, d):
        return index > 0 if d else index < last

    barrier = pltpu.get_barrier_semaphore()

    def greet(device):
        pl.semaphore_signal(barrier, inc=1, device_id=device, device_id_type=MESH)

    def gx_device(i):
        return (lax.rem(g + i, 16), l, q)

    far = jnp.logical_or(q == 1, q == 2)
    for i in (1, 15):
        greet(gx_device(i))
        greet(ring_device(lax.rem(ring + i, 16)))
    greet((g, l, partner))

    @pl.when(far)
    def _():
        greet((g, l, 3 - q))

    for x in range(12):
        load(x).start()
    small = [
        pltpu.make_async_copy(src, dst, small_sem.at[i])
        for i, (src, dst) in enumerate((
            (speeds_hbm, SPD), (kin_hbm, KIN), (rank_hbm, RANK), (xf_hbm, XF),
            (yf_hbm, YF), (zf_hbm, ZT.at[pl.ds(0, 54)]),
        ))
    ]
    YT[...] = jnp.zeros((8, 128), f32)
    ZT[...] = jnp.zeros((128, 128), f32)
    ZX[pl.ds(136, 120)] = jnp.zeros((120, 128), f32)
    for copy in small:
        copy.start()

    def tell(n):
        for i in (1 << n, 16 - (1 << n)):
            pl.semaphore_signal(gx_round.at[n], inc=1, device_id=gx_device(i), device_id_type=MESH)
            pl.semaphore_signal(z_round.at[n], inc=1, device_id=ring_device(lax.rem(ring + i, 16)),
                                device_id_type=MESH)

    def hear(n):
        pl.semaphore_wait(gx_round.at[n], 2)
        pl.semaphore_wait(z_round.at[n], 2)

    for d in range(2):
        rows = pl.ds(4 * d, 4)

        @pl.when(jnp.logical_not(can_recv(l, 7, d)))
        def _():
            YB[:, :, :, rows, :] = jnp.zeros((2, 12, 16, 4, 128), f32)

        @pl.when(jnp.logical_not(can_recv(q, 3, d)))
        def _():
            ZB[:, :, rows, :] = jnp.zeros((2, 12, 4, 128), f32)
            ZX[pl.ds(128 + 4 * d, 4)] = jnp.zeros((4, 128), f32)

        @pl.when(jnp.logical_not(can_recv(g, 15, d)))
        def _():
            for X in (FX, SX):
                X[pl.ds(0 if d else 16, 4)] = jnp.zeros((4, 16, 8, 128), f32)

    i8, c8 = iota((8, 256), 0), jnp.bitwise_and(iota((8, 256), 1), 127)
    SEL[...] = onehot(c8 == jnp.where(i8 < 4, i8, 120 + i8))
    for x in range(12):
        load(x).wait()

    def first_z(x, c):
        p = jnp.where(lax.rem(x, 2) == 1, 6 + x // 2, 5 - x // 2)
        ZS[0, x] = dot(SEL[...], both(FX[4 + p].reshape(128, 128)), NT)
        return c

    lax.fori_loop(0, 12, first_z, 0)
    for copy in small:
        copy.wait()
    ZX[pl.ds(0, 128)] = ZT[...].T
    ZE[pl.ds(0, 4)] = ZX[pl.ds(0, 4)]
    ZE[pl.ds(4, 4)] = ZX[pl.ds(124, 4)]
    pl.semaphore_wait(barrier, 5 + jnp.where(far, 1, 0))
    for d in range(2):
        pl.when(can_send(q, 3, d))(lambda: z0copy(d).start())
        pl.when(can_send(q, 3, d))(lambda: zfcopy(d).start())

    def send_edges(j, c):
        for p in (5 - j, 6 + j):
            for d in range(2):
                pl.when(can_send(l, 7, d))(lambda: ycopy(0, d, p).start())
        return c

    def send_planes(i, c):
        pl.when(can_send(g, 15, 1))(lambda: xcopy(0, 1, 3 - i).start())
        pl.when(can_send(g, 15, 0))(lambda: xcopy(0, 0, i).start())
        return c

    lax.fori_loop(0, 2, send_edges, 0)
    lax.fori_loop(0, 4, send_planes, 0)
    lax.fori_loop(2, 6, send_edges, 0)
    tell(0)

    row, col = iota((128, 256), 0), iota((128, 256), 1)
    v, y = row >> 3, jnp.bitwise_and(row, 7)
    own = col < 128
    cc = jnp.bitwise_and(col, 127)
    w, s8 = cc >> 3, jnp.bitwise_and(cc, 7)
    y2 = jnp.where(own, s8, jnp.where(s8 < 4, 8 + s8, s8 - 8))
    rows_v = onehot(iota((128, 16), 0) >> 3 == iota((128, 16), 1))
    cols_w = onehot(jnp.bitwise_and(iota((16, 256), 1), 127) >> 3 == iota((16, 256), 0))

    def spread(value):
        total = jnp.zeros((128, 256), f32)
        for part in split(value):
            total = total + dot(dot(rows_v, part).astype(bf16), cols_w)
        return total

    lane = iota((16, 16), 1) == iota((16, 16), 0)

    def speed_rows(d):
        total = jnp.zeros((128, 256), f32)
        for part in split(jnp.where(lane, SPD[d : d + 1, :], 0.0)):
            total = total + dot(rows_v, dot(part, jnp.ones((16, 256), bf16)).astype(bf16))
        return -TIME_STEP * total

    SXR[...] = speed_rows(0)[:, :128]
    SZR[...] = speed_rows(2)[:, :128]
    A = jnp.where(y == y2, TIME_STEP * spread(KIN[...]), 0.0)
    K2[...] = stacked(A[:, :128])
    A = A + jnp.where(v == w, speed_rows(1) * stencil(y2 - y), 0.0)
    A2[...] = jnp.concatenate(split(A), axis=0)
    D = both(stencil(iota((128, 128), 0) - iota((128, 128), 1)))
    D2[...] = jnp.concatenate([D, D], axis=0)
    i8, z8 = iota((8, 128), 0), iota((8, 128), 1)
    E = both(stencil(jnp.where(i8 < 4, 128 + i8, i8 - 8) - z8))
    E2[...] = jnp.concatenate([E, E], axis=0)
    XR[...] = jnp.zeros((16, 128), f32)
    for i in range(12):
        XR[i : i + 1, 0:96] = XF[pl.ds(RANK[6 + i // 2 if i % 2 else 5 - i // 2], 1), :]
    YT[:, 0:64] = YF[...]
    XG[g] = XR[...]
    YG[l] = YT[...]

    def xrow(peer, slot):
        return remote(XR, XG.at[slot], xrs.at[peer], xrr.at[slot], (peer, l, q))

    def yrow(peer, slot):
        return remote(YT, YG.at[slot], yrs.at[peer], yrr.at[slot], (g, peer, q))

    def over(n, me, act):
        def body(i, c):
            act(lax.rem(me + i, n))
            return c
        lax.fori_loop(1, n, body, 0)

    hear(0)
    tell(1)
    hear(1)
    tell(2)

    def change(X, s, p, place):
        center = X[4 + p].reshape(128, 128)
        F = jnp.concatenate([both(center), both(YB[s, p].reshape(128, 128))], axis=0)
        t = dot(A2[...], F)
        zt = dot(F[:128], D2[...])
        zt = zt + dot(jnp.concatenate(split(ZB[s, place]), axis=0), E2[...], TN)
        xt = jnp.zeros((16, 8, 128), f32)
        for i, c in enumerate(COEFFS):
            xt = xt + c * (X[5 + i + p] - X[3 - i + p])
        return center, quadrants(t) + SZR[...] * halves(zt) + SXR[...] * xt.reshape(128, 128)

    def wait_halo(j, s):
        for p in (5 - j, 6 + j):
            for d in range(2):
                pl.when(can_recv(l, 7, d))(lambda: ycopy(s, d, p).wait_recv())
        for d in range(2):
            if s:
                pl.when(can_recv(q, 3, d))(lambda: zcopy(d, j).wait_recv())
            i = 5 - j if d else j - 2
            pl.when(jnp.logical_and(j >= 2, can_recv(g, 15, d)))(
                lambda: xcopy(s, d, i).wait_recv())

    for d in range(2):
        pl.when(can_recv(q, 3, d))(lambda: z0copy(d).wait_recv())
        pl.when(can_recv(q, 3, d))(lambda: zfcopy(d).wait_recv())

    row, col = iota((128, 256), 0), iota((128, 256), 1)
    Z = ZX[pl.ds(0, 128)]
    DZ = product(stencil(row - jnp.where(col < 132, col, col - 136)), ZX[...])
    for n, a in enumerate((Z, DZ)):
        Z2[256 * n : 256 * n + 256, :] = both(jnp.concatenate([a, pltpu.roll(a, 64, 1)], axis=0))

    def first(j, c):
        @pl.when(j == 4)
        def _():
            hear(2)
            over(16, g, lambda peer: xrow(peer, g).start())
            over(8, l, lambda peer: yrow(peer, l).start())

        wait_halo(j, 0)
        for i, p in enumerate((5 - j, 6 + j)):
            center, add = change(FX, 0, p, 2 * j + i)
            section = center + add
            SX[4 + p] = section.reshape(16, 8, 128)
            parts = both(section)
            ZS[1, 2 * j + i] = dot(SEL[...], parts, NT)
            mixed = 0.5 * (FX[4 + p].reshape(128, 128) + section + quadrants(dot(K2[...], parts)))
            both_z = jnp.concatenate([paired(mixed), paired(0.5 * SZR[...] * section)], axis=1)
            z0 = quadrants(dot(stacked(both_z), Z2[...])).reshape(2, 2, 2, 8, 128)
            z1 = quadrants(dot(stacked(paired(section)), Z2[0:256, :])).reshape(2, 2, 2, 8, 128)
            for n in range(2):
                PB[n, 2 * j + i, 0] = z0[:, n].reshape(4, 8, 128)
                PB[n, 2 * j + i, 1] = z1[:, n].reshape(4, 8, 128)
        bcopy(j).start()
        for d in range(2):
            pl.when(can_send(q, 3, d))(lambda: zcopy(d, j).start())
        for p in (5 - j, 6 + j):
            for d in range(2):
                pl.when(can_send(l, 7, d))(lambda: ycopy(1, d, p).start())
        return c

    def projections():
        over(16, g, lambda peer: xrow(peer, peer).wait_recv())
        over(8, l, lambda peer: yrow(peer, peer).wait_recv())
        shape = (4, 12, 8, 256)
        src = 4 * iota(shape, 0) + (iota(shape, 2) >> 1)
        pick = onehot((16 * src + iota(shape, 1) == iota(shape, 3)).reshape(384, 256))
        shape = (6, 4, 8, 128)
        rank = 24 * iota(shape, 1) + 6 * (iota(shape, 2) >> 1) + iota(shape, 0)
        ranks = onehot((rank == iota(shape, 3)).reshape(192, 128))
        same = jnp.bitwise_and(iota((192, 384), 0) ^ iota((192, 384), 1), 1) == 0
        def plane(index):
            step, n = jnp.bitwise_and(index, 15) >> 1, jnp.bitwise_and(index, 1)
            return 12 * (index >> 4) + jnp.where(n == 1, 6 + step, 5 - step)

        X = XG[...].reshape(256, 128)
        DX = product(stencil(plane(iota((256, 256), 0)) - plane(iota((256, 256), 1))), X)
        for m, a in enumerate((X, DX)):
            for n, part in enumerate(split(a)):
                rows = dot(ranks, dot(pick, part).astype(bf16), NT)
                X2[192 * n : 192 * n + 192, 384 * m : 384 * m + 384] = jnp.where(same, rows, 0.0).astype(bf16)
        Y = YG[...].reshape(64, 128)
        Y = Y + pltpu.roll(Y, 64, 1)
        DY = product(stencil(iota((64, 64), 0) - iota((64, 64), 1)), Y)
        col = iota((64, 256), 1)
        pick = onehot(8 * jnp.bitwise_and(col >> 4, 7) + jnp.bitwise_and(col, 7) == iota((64, 256), 0))
        same = iota((128, 256), 0) >> 6 == jnp.bitwise_and(iota((128, 256), 1) >> 3, 1)
        for m, a in enumerate((Y, DY)):
            for n, part in enumerate(split(a)):
                W2[128 * n : 128 * n + 128, 256 * m : 256 * m + 256] = (
                    jnp.where(same, dot(part, pick, TN), 0.0).astype(bf16))

    def put(p):
        return pltpu.make_async_copy(FN.at[p], next_ref.at[:, p], out_sem.at[p])

    def place(d):
        return d // 4, pl.ds(2 * lax.rem(d, 4), 2)

    def ccopy(n, peer, slot):
        t, rows = place(peer)
        t2, rows2 = place(slot)
        part = pl.ds(8 * n, 8 - 4 * n)
        return remote(QB.at[part, :, t, rows], CT.at[t2, part, :, rows2], csend.at[n, peer],
                      crecv.at[n, slot], (peer, l, q))

    def send_part(n):
        def add_partner(x, c):
            bcopy(x).wait_recv()
            pair = pl.ds(2 * x, 2)
            QB[pair] = PB[k, pair] + BR[pair]
            return c

        lax.fori_loop(4 * n, 4 + 2 * n, add_partner, 0)
        over(16, g, lambda peer: ccopy(n, peer, g).start())

    def second(j, c):
        wait_halo(j, 1)
        for i, p in enumerate((5 - j, 6 + j)):
            center, add = change(SX, 1, p, 2 * j + i)
            new = 0.5 * (FX[4 + p].reshape(128, 128) + center + add)
            FN[p] = new.reshape(16, 8, 128)
            put(p).start()
        return c

    lax.fori_loop(0, 5, first, 0)
    send_part(0)
    first(5, 0)

    send_part(1)
    projections()

    def ecopy(peer, slot):
        t, rows = place(peer)
        t2, rows2 = place(slot)
        return remote(RB.at[:, :, t, rows], EU.at[:, t2, :, rows2], esend.at[peer], erecv.at[slot],
                      (peer, l, q))

    t, rows = place(g)
    mine = pltpu.make_async_copy(QB.at[:, :, t, rows], CT.at[t, :, :, rows], own_sem.at[0])
    mine.start()
    mine.wait()
    for n in range(2):
        over(16, g, lambda peer: ccopy(n, peer, peer).wait_recv())
    v0 = 8 * (t // 2) + 4 * k + 2 * lax.rem(t, 2)

    def lane_speeds(d):
        which = iota((1, 16), 1)
        pair = [jnp.sum(jnp.where(which == v0 + n, SPD[d : d + 1, :], 0.0), axis=1, keepdims=True)
                for n in range(2)]
        return -0.5 * TIME_STEP * jnp.where(iota((1, 128), 1) < 64, pair[0], pair[1])

    T0, T1 = CT[:, :, 0].reshape(384, 128), CT[:, :, 1].reshape(384, 128)
    R0 = quadrants(dot(X2[...], both(jnp.concatenate([T0, lane_speeds(0) * T1], axis=0))))
    R1 = quadrants(dot(X2[:, 0:384], both(lane_speeds(1) * T1)))
    RB[0] = R0.reshape(6, 4, 8, 128)
    RB[1] = R1.reshape(6, 4, 8, 128)
    over(16, g, lambda peer: ecopy(peer, g).start())

    def send_sections(i, c):
        pl.when(can_send(g, 15, 1))(lambda: xcopy(1, 1, 3 - i).start())
        pl.when(can_send(g, 15, 0))(lambda: xcopy(1, 0, i).start())
        return c

    lax.fori_loop(0, 4, send_sections, 0)
    mine = pltpu.make_async_copy(RB.at[:, :, t, rows], EU.at[:, t, :, rows], own_sem.at[1])
    mine.start()
    mine.wait()
    lax.fori_loop(0, 2, second, 0)
    over(16, g, lambda peer: ecopy(peer, peer).wait_recv())

    def unit(r):
        n = lax.rem(r, 8) - 1
        return 2 * (r // 8) + n // 3, pl.ds(2 * lax.rem(n, 3), 2)

    def working(r):
        return jnp.logical_and(lax.rem(r, 8) >= 1, lax.rem(r, 8) <= 6)

    def fcopy(r):
        t, ranks = unit(r)
        return remote(EU.at[:, t, ranks], FU.at[ring], fsend.at[r], frecv.at[ring], ring_device(r))

    def fcome(r):
        return remote(EU.at[:, 0, pl.ds(0, 2)], FU.at[r], fsend.at[r], frecv.at[r], ring_device(r))

    def send_unit(i, c):
        r = lax.rem(ring + jnp.where(lax.rem(i, 2) == 0, 8 + i // 2, 7 - i // 2), 16)
        pl.when(working(r))(lambda: fcopy(r).start())
        return c

    lax.fori_loop(0, 15, send_unit, 0)
    works = working(ring)

    @pl.when(works)
    def _():
        t, ranks = unit(ring)
        mine = pltpu.make_async_copy(EU.at[:, t, ranks], FU.at[ring], own_sem.at[0])
        mine.start()
        mine.wait()

    def gcopy(there, slot):
        return remote(SB.at[:, there], GB.at[slot], gsend.at[there], grecv.at[slot], (g, there, q))

    lax.fori_loop(2, 6, second, 0)

    @pl.when(works)
    def _():
        over(16, ring, lambda r: fcome(r).wait_recv())
        U = [FU[:, n].reshape(256, 128) for n in range(2)]
        S = quadrants(dot(W2[...], both(jnp.concatenate(U, axis=0))))
        SB[...] = S.reshape(2, 8, 8, 128)
        over(8, l, lambda there: gcopy(there, l - 1).start())
        GB[l - 1] = SB[:, l]

    def done(p, c):
        for s in range(2):
            for d in range(2):
                pl.when(can_send(l, 7, d))(lambda: ycopy(s, d, p).wait_send())
        put(p).wait()
        return c

    lax.fori_loop(0, 12, done, 0)
    for j in range(6):
        bcopy(j).wait_send()
        for d in range(2):
            pl.when(can_send(q, 3, d))(lambda: zcopy(d, j).wait_send())
    for d in range(2):
        pl.when(can_send(q, 3, d))(lambda: z0copy(d).wait_send())
        pl.when(can_send(q, 3, d))(lambda: zfcopy(d).wait_send())
        for s in range(2):
            for i in range(4):
                pl.when(can_send(g, 15, d))(lambda: xcopy(s, d, i).wait_send())

    def done_peer(peer):
        xrow(peer, g).wait_send()
        for n in range(2):
            ccopy(n, peer, g).wait_send()
        ecopy(peer, g).wait_send()

    over(16, g, done_peer)
    over(8, l, lambda peer: yrow(peer, l).wait_send())
    over(16, ring, lambda r: pl.when(working(r))(lambda: fcopy(r).wait_send()))

    for e in range(6):
        pl.when(l != e + 1)(lambda: gcopy(l, e).wait_recv())
    for u in range(2):
        for a in range(6):
            tile = GB[3 * u + a // 2, a % 2]
            core_ref[2 * u, a] = tile[:, 0:54]
            core_ref[2 * u + 1, a] = pltpu.roll(tile, 64, 1)[:, 0:54]

    @pl.when(works)
    def _():
        over(8, l, lambda there: gcopy(there, l - 1).wait_send())


def local(fields, speeds, kinetics, block_rank, x_factor, y_factor, z_factor):
    vmem, dma = pltpu.VMEM, pltpu.SemaphoreType.DMA
    in_vmem = pl.BlockSpec(memory_space=pltpu.VMEM)
    in_hbm = pl.BlockSpec(memory_space=pltpu.HBM)
    return pl.pallas_call(
        kernel,
        out_shape=(
            jax.ShapeDtypeStruct(fields.shape, f32),
            jax.ShapeDtypeStruct((4, 6, 8, 54), f32),
        ),
        in_specs=[in_hbm] * 7,
        out_specs=(in_hbm, in_vmem),
        scratch_shapes=[
            vmem((20, 16, 8, 128), f32),
            vmem((20, 16, 8, 128), f32),
            vmem((2, 12, 16, 8, 128), f32),
            vmem((2, 12, 8, 128), f32),
            vmem((2, 12, 8, 128), f32),
            vmem((12, 16, 8, 128), f32),
            vmem((2, 12, 2, 4, 8, 128), f32),
            vmem((12, 2, 4, 8, 128), f32),
            vmem((12, 2, 4, 8, 128), f32),
            vmem((4, 12, 2, 8, 128), f32),
            vmem((2, 6, 4, 8, 128), f32),
            vmem((2, 4, 6, 8, 128), f32),
            vmem((16, 2, 2, 8, 128), f32),
            vmem((2, 8, 8, 128), f32),
            vmem((6, 2, 8, 128), f32),
            vmem((16, 128), f32),
            vmem((16, 16, 128), f32),
            vmem((8, 128), f32),
            vmem((8, 8, 128), f32),
            vmem((128, 128), f32),
            vmem((8, 128), f32),
            vmem((256, 128), f32),
            vmem((192, 96), f32),
            vmem((8, 64), f32),
            vmem((16, 16), f32),
            vmem((3, 16), f32),
            pltpu.SMEM((12,), jnp.int32),
            vmem((256, 256), bf16),
            vmem((256, 128), bf16),
            vmem((256, 256), bf16),
            vmem((16, 256), bf16),
            vmem((8, 256), bf16),
            vmem((512, 256), bf16),
            vmem((384, 768), bf16),
            vmem((256, 512), bf16),
            vmem((128, 128), f32),
            vmem((128, 128), f32),
            dma((12,)), dma((6,)), dma((12,)), dma((2,)),
            dma((2, 2, 12)), dma((2, 2, 12)),
            dma((2, 6)), dma((2, 6)), dma((2,)), dma((2,)), dma((2,)), dma((2,)),
            dma((2, 2, 4)), dma((2, 2, 4)),
            dma((6,)), dma((6,)),
            dma((2, 16)), dma((2, 16)), dma((16,)), dma((16,)), dma((16,)), dma((16,)),
            dma((8,)), dma((8,)),
            dma((16,)), dma((16,)), dma((8,)), dma((8,)),
            pltpu.SemaphoreType.REGULAR((3,)), pltpu.SemaphoreType.REGULAR((3,)),
        ],
        compiler_params=pltpu.CompilerParams(
            collective_id=0, has_side_effects=True, vmem_limit_bytes=60 * 1024 * 1024),
    )(fields, speeds, kinetics, block_rank, x_factor, y_factor, z_factor.T)


def solution(mesh):
    placed = (P(None, "gx", "gy", "gz"), P(), P(), P("gx"), P(), P("gy", None), P("gz", None))
    return jax.shard_map(
        local,
        mesh=mesh,
        in_specs=placed,
        out_specs=(P(None, "gx", "gy", "gz"), P("gz", "gx", "gy", None)),
        check_vma=False,
    )
```

```python
import jax
import jax.numpy as jnp
from jax import lax
from jax.experimental import pallas as pl
from jax.experimental.pallas import tpu as pltpu
from jax.sharding import PartitionSpec as P

COEFFS = (0.8, -0.2, 4.0 / 105.0, -1.0 / 280.0)
TIME_STEP = 0.45
MESH = pl.DeviceIdType.MESH
f32, bf16 = jnp.float32, jnp.bfloat16
NN = (((1,), (0,)), ((), ()))
NT = (((1,), (1,)), ((), ()))
TN = (((0,), (0,)), ((), ()))


def dot(a, b, dims=NN):
    return lax.dot_general(a, b, dims, preferred_element_type=f32)


def split(a):
    high = a.astype(bf16)
    return high, (a - high.astype(f32)).astype(bf16)


def iota(shape, dim):
    return lax.broadcasted_iota(jnp.int32, shape, dim)


def onehot(mask):
    return jnp.where(mask, 1.0, 0.0).astype(bf16)


def stencil(offset):
    value = jnp.zeros(offset.shape, f32)
    for k, c in enumerate(COEFFS):
        value = jnp.where(offset == k + 1, c, value)
        value = jnp.where(offset == -k - 1, -c, value)
    return value


def quadrants(t):
    m, n = t.shape[0] // 2, t.shape[1] // 2
    return t[:m, :n] + (t[m:, :n] + t[:m, n:])


def halves(t):
    n = t.shape[1] // 2
    return t[:, :n] + t[:, n:]


def both(a):
    return jnp.concatenate(split(a), axis=1)


def stacked(a):
    return jnp.concatenate(split(a), axis=0)


def product(a, b):
    return quadrants(dot(stacked(a), both(b)))


def paired(a):
    a = a.reshape(8, 2, 8, 128)
    return jnp.concatenate([a[:, 0].reshape(64, 128), a[:, 1].reshape(64, 128)], axis=1)


def kernel(
    f_hbm, speeds_hbm, kin_hbm, rank_hbm, xf_hbm, yf_hbm, zf_hbm,
    next_ref, core_ref,
    FX, SX, YB, ZS, ZB, FN, PB, BR, QB, CT, RB, EU, FU, SB, GB, XR, XG, YT, YG, ZT, ZE, ZX, XF, YF, KIN, SPD, RANK,
    A2, K2, D2, E2, SEL, Z2, X2, W2, SXR, SZR,
    load_sem, small_sem, out_sem, own_sem, ysend, yrecv, zsend, zrecv, z0send, z0recv, zfsend, zfrecv, xsend, xrecv,
    bsend, brecv, csend, crecv, esend, erecv, fsend, frecv, gsend, grecv,
    xrs, xrr, yrs, yrr, gx_round, z_round,
):
    g, l, q = lax.axis_index("gx"), lax.axis_index("gy"), lax.axis_index("gz")
    h, k = q // 2, lax.rem(q, 2)
    ring = h * 8 + l
    partner = q + 1 - 2 * k

    def ring_device(r):
        return (g, lax.rem(r, 8), 2 * (r // 8) + k)

    def remote(src, dst, send, recv, device):
        return pltpu.make_async_remote_copy(
            src_ref=src, dst_ref=dst, send_sem=send, recv_sem=recv,
            device_id=device, device_id_type=MESH)

    def load(x):
        return pltpu.make_async_copy(f_hbm.at[:, x], FX.at[4 + x], load_sem.at[x])

    def ycopy(s, d, p):
        X = (FX, SX)[s]
        rows = pl.ds(4 * d, 4)
        return remote(X.at[4 + p, :, rows], YB.at[s, p, :, rows], ysend.at[s, d, p],
                      yrecv.at[s, d, p], (g, l + 2 * d - 1, q))

    def z0copy(d):
        rows = pl.ds(4 * d, 4)
        return remote(ZS.at[0, :, rows], ZB.at[0, :, rows], z0send.at[d], z0recv.at[d],
                      (g, l, q + 2 * d - 1))

    def zfcopy(d):
        return remote(ZE.at[pl.ds(4 * d, 4)], ZX.at[pl.ds(128 + 4 * d, 4)], zfsend.at[d], zfrecv.at[d],
                      (g, l, q + 2 * d - 1))

    def zcopy(d, j):
        rows, pair = pl.ds(4 * d, 4), pl.ds(2 * j, 2)
        return remote(ZS.at[1, pair, rows], ZB.at[1, pair, rows], zsend.at[d, j], zrecv.at[d, j],
                      (g, l, q + 2 * d - 1))

    def xcopy(s, d, i):
        X = (FX, SX)[s]
        src, dst = (12 + i, i) if d else (4 + i, 16 + i)
        return remote(X.at[src], X.at[dst], xsend.at[s, d, i], xrecv.at[s, d, i],
                      (g + 2 * d - 1, l, q))

    def bcopy(x):
        pair = pl.ds(2 * x, 2)
        return remote(PB.at[1 - k, pair], BR.at[pair], bsend.at[x], brecv.at[x], (g, l, partner))

    def can_send(index, last, d):
        return index < last if d else index > 0

    def can_recv(index, last, d):
        return index > 0 if d else index < last

    barrier = pltpu.get_barrier_semaphore()

    def greet(device):
        pl.semaphore_signal(barrier, inc=1, device_id=device, device_id_type=MESH)

    def gx_device(i):
        return (lax.rem(g + i, 16), l, q)

    far = jnp.logical_or(q == 1, q == 2)
    for i in (1, 15):
        greet(gx_device(i))
        greet(ring_device(lax.rem(ring + i, 16)))
    greet((g, l, partner))

    @pl.when(far)
    def _():
        greet((g, l, 3 - q))

    for x in range(12):
        load(x).start()
    small = [
        pltpu.make_async_copy(src, dst, small_sem.at[i])
        for i, (src, dst) in enumerate((
            (speeds_hbm, SPD), (kin_hbm, KIN), (rank_hbm, RANK), (xf_hbm, XF),
            (yf_hbm, YF), (zf_hbm, ZT.at[pl.ds(0, 54)]),
        ))
    ]
    YT[...] = jnp.zeros((8, 128), f32)
    ZT[...] = jnp.zeros((128, 128), f32)
    ZX[pl.ds(136, 120)] = jnp.zeros((120, 128), f32)
    for copy in small:
        copy.start()

    def tell(n):
        for i in (1 << n, 16 - (1 << n)):
            pl.semaphore_signal(gx_round.at[n], inc=1, device_id=gx_device(i), device_id_type=MESH)
            pl.semaphore_signal(z_round.at[n], inc=1, device_id=ring_device(lax.rem(ring + i, 16)),
                                device_id_type=MESH)

    def hear(n):
        pl.semaphore_wait(gx_round.at[n], 2)
        pl.semaphore_wait(z_round.at[n], 2)

    for d in range(2):
        rows = pl.ds(4 * d, 4)

        @pl.when(jnp.logical_not(can_recv(l, 7, d)))
        def _():
            YB[:, :, :, rows, :] = jnp.zeros((2, 12, 16, 4, 128), f32)

        @pl.when(jnp.logical_not(can_recv(q, 3, d)))
        def _():
            ZB[:, :, rows, :] = jnp.zeros((2, 12, 4, 128), f32)
            ZX[pl.ds(128 + 4 * d, 4)] = jnp.zeros((4, 128), f32)

        @pl.when(jnp.logical_not(can_recv(g, 15, d)))
        def _():
            for X in (FX, SX):
                X[pl.ds(0 if d else 16, 4)] = jnp.zeros((4, 16, 8, 128), f32)

    i8, c8 = iota((8, 256), 0), jnp.bitwise_and(iota((8, 256), 1), 127)
    SEL[...] = onehot(c8 == jnp.where(i8 < 4, i8, 120 + i8))
    for x in range(12):
        load(x).wait()

    def first_z(x, c):
        p = jnp.where(lax.rem(x, 2) == 1, 6 + x // 2, 5 - x // 2)
        ZS[0, x] = dot(SEL[...], both(FX[4 + p].reshape(128, 128)), NT)
        return c

    lax.fori_loop(0, 12, first_z, 0)
    for copy in small:
        copy.wait()
    ZX[pl.ds(0, 128)] = ZT[...].T
    ZE[pl.ds(0, 4)] = ZX[pl.ds(0, 4)]
    ZE[pl.ds(4, 4)] = ZX[pl.ds(124, 4)]
    pl.semaphore_wait(barrier, 5 + jnp.where(far, 1, 0))
    for d in range(2):
        pl.when(can_send(q, 3, d))(lambda: z0copy(d).start())
        pl.when(can_send(q, 3, d))(lambda: zfcopy(d).start())

    def send_edges(j, c):
        for p in (5 - j, 6 + j):
            for d in range(2):
                pl.when(can_send(l, 7, d))(lambda: ycopy(0, d, p).start())
        return c

    def send_planes(i, c):
        pl.when(can_send(g, 15, 1))(lambda: xcopy(0, 1, 3 - i).start())
        pl.when(can_send(g, 15, 0))(lambda: xcopy(0, 0, i).start())
        return c

    lax.fori_loop(0, 2, send_edges, 0)
    lax.fori_loop(0, 4, send_planes, 0)
    lax.fori_loop(2, 6, send_edges, 0)
    tell(0)

    row, col = iota((128, 256), 0), iota((128, 256), 1)
    v, y = row >> 3, jnp.bitwise_and(row, 7)
    own = col < 128
    cc = jnp.bitwise_and(col, 127)
    w, s8 = cc >> 3, jnp.bitwise_and(cc, 7)
    y2 = jnp.where(own, s8, jnp.where(s8 < 4, 8 + s8, s8 - 8))
    rows_v = onehot(iota((128, 16), 0) >> 3 == iota((128, 16), 1))
    cols_w = onehot(jnp.bitwise_and(iota((16, 256), 1), 127) >> 3 == iota((16, 256), 0))

    def spread(value):
        total = jnp.zeros((128, 256), f32)
        for part in split(value):
            total = total + dot(dot(rows_v, part).astype(bf16), cols_w)
        return total

    lane = iota((16, 16), 1) == iota((16, 16), 0)

    def speed_rows(d):
        total = jnp.zeros((128, 256), f32)
        for part in split(jnp.where(lane, SPD[d : d + 1, :], 0.0)):
            total = total + dot(rows_v, dot(part, jnp.ones((16, 256), bf16)).astype(bf16))
        return -TIME_STEP * total

    SXR[...] = speed_rows(0)[:, :128]
    SZR[...] = speed_rows(2)[:, :128]
    A = jnp.where(y == y2, TIME_STEP * spread(KIN[...]), 0.0)
    K2[...] = stacked(A[:, :128])
    A = A + jnp.where(v == w, speed_rows(1) * stencil(y2 - y), 0.0)
    A2[...] = jnp.concatenate(split(A), axis=0)
    D = both(stencil(iota((128, 128), 0) - iota((128, 128), 1)))
    D2[...] = jnp.concatenate([D, D], axis=0)
    i8, z8 = iota((8, 128), 0), iota((8, 128), 1)
    E = both(stencil(jnp.where(i8 < 4, 128 + i8, i8 - 8) - z8))
    E2[...] = jnp.concatenate([E, E], axis=0)
    XR[...] = jnp.zeros((16, 128), f32)
    for i in range(12):
        XR[i : i + 1, 0:96] = XF[pl.ds(RANK[6 + i // 2 if i % 2 else 5 - i // 2], 1), :]
    YT[:, 0:64] = YF[...]
    XG[g] = XR[...]
    YG[l] = YT[...]

    def xrow(peer, slot):
        return remote(XR, XG.at[slot], xrs.at[peer], xrr.at[slot], (peer, l, q))

    def yrow(peer, slot):
        return remote(YT, YG.at[slot], yrs.at[peer], yrr.at[slot], (g, peer, q))

    def over(n, me, act):
        def body(i, c):
            act(lax.rem(me + n // 2 + jnp.where(lax.rem(i, 2) == 0, i // 2, -((i + 1) // 2)), n))
            return c
        lax.fori_loop(0, n - 1, body, 0)

    hear(0)
    tell(1)
    hear(1)
    tell(2)

    def change(X, s, p, place):
        center = X[4 + p].reshape(128, 128)
        F = jnp.concatenate([both(center), both(YB[s, p].reshape(128, 128))], axis=0)
        t = dot(A2[...], F)
        zt = dot(F[:128], D2[...])
        zt = zt + dot(jnp.concatenate(split(ZB[s, place]), axis=0), E2[...], TN)
        xt = jnp.zeros((16, 8, 128), f32)
        for i, c in enumerate(COEFFS):
            xt = xt + c * (X[5 + i + p] - X[3 - i + p])
        return center, quadrants(t) + SZR[...] * halves(zt) + SXR[...] * xt.reshape(128, 128)

    def wait_halo(j, s):
        for p in (5 - j, 6 + j):
            for d in range(2):
                pl.when(can_recv(l, 7, d))(lambda: ycopy(s, d, p).wait_recv())
        for d in range(2):
            if s:
                pl.when(can_recv(q, 3, d))(lambda: zcopy(d, j).wait_recv())
            i = 5 - j if d else j - 2
            pl.when(jnp.logical_and(j >= 2, can_recv(g, 15, d)))(
                lambda: xcopy(s, d, i).wait_recv())

    for d in range(2):
        pl.when(can_recv(q, 3, d))(lambda: z0copy(d).wait_recv())
        pl.when(can_recv(q, 3, d))(lambda: zfcopy(d).wait_recv())

    row, col = iota((128, 256), 0), iota((128, 256), 1)
    Z = ZX[pl.ds(0, 128)]
    DZ = product(stencil(row - jnp.where(col < 132, col, col - 136)), ZX[...])
    for n, a in enumerate((Z, DZ)):
        Z2[256 * n : 256 * n + 256, :] = both(jnp.concatenate([a, pltpu.roll(a, 64, 1)], axis=0))

    def first(j, c):
        @pl.when(j == 4)
        def _():
            hear(2)
            over(16, g, lambda peer: xrow(peer, g).start())
            over(8, l, lambda peer: yrow(peer, l).start())

        wait_halo(j, 0)
        for i, p in enumerate((5 - j, 6 + j)):
            center, add = change(FX, 0, p, 2 * j + i)
            section = center + add
            SX[4 + p] = section.reshape(16, 8, 128)
            parts = both(section)
            ZS[1, 2 * j + i] = dot(SEL[...], parts, NT)
            mixed = 0.5 * (FX[4 + p].reshape(128, 128) + section + quadrants(dot(K2[...], parts)))
            both_z = jnp.concatenate([paired(mixed), paired(0.5 * SZR[...] * section)], axis=1)
            z0 = quadrants(dot(stacked(both_z), Z2[...])).reshape(2, 2, 2, 8, 128)
            z1 = quadrants(dot(stacked(paired(section)), Z2[0:256, :])).reshape(2, 2, 2, 8, 128)
            for n in range(2):
                PB[n, 2 * j + i, 0] = z0[:, n].reshape(4, 8, 128)
                PB[n, 2 * j + i, 1] = z1[:, n].reshape(4, 8, 128)
        bcopy(j).start()
        for d in range(2):
            pl.when(can_send(q, 3, d))(lambda: zcopy(d, j).start())
        for p in (5 - j, 6 + j):
            for d in range(2):
                pl.when(can_send(l, 7, d))(lambda: ycopy(1, d, p).start())
        return c

    def projections():
        over(16, g, lambda peer: xrow(peer, peer).wait_recv())
        over(8, l, lambda peer: yrow(peer, peer).wait_recv())
        shape = (4, 12, 8, 256)
        src = 4 * iota(shape, 0) + (iota(shape, 2) >> 1)
        pick = onehot((16 * src + iota(shape, 1) == iota(shape, 3)).reshape(384, 256))
        shape = (6, 4, 8, 128)
        rank = 24 * iota(shape, 1) + 6 * (iota(shape, 2) >> 1) + iota(shape, 0)
        ranks = onehot((rank == iota(shape, 3)).reshape(192, 128))
        same = jnp.bitwise_and(iota((192, 384), 0) ^ iota((192, 384), 1), 1) == 0
        def plane(index):
            step, n = jnp.bitwise_and(index, 15) >> 1, jnp.bitwise_and(index, 1)
            return 12 * (index >> 4) + jnp.where(n == 1, 6 + step, 5 - step)

        X = XG[...].reshape(256, 128)
        DX = product(stencil(plane(iota((256, 256), 0)) - plane(iota((256, 256), 1))), X)
        for m, a in enumerate((X, DX)):
            for n, part in enumerate(split(a)):
                rows = dot(ranks, dot(pick, part).astype(bf16), NT)
                X2[192 * n : 192 * n + 192, 384 * m : 384 * m + 384] = jnp.where(same, rows, 0.0).astype(bf16)
        Y = YG[...].reshape(64, 128)
        Y = Y + pltpu.roll(Y, 64, 1)
        DY = product(stencil(iota((64, 64), 0) - iota((64, 64), 1)), Y)
        col = iota((64, 256), 1)
        pick = onehot(8 * jnp.bitwise_and(col >> 4, 7) + jnp.bitwise_and(col, 7) == iota((64, 256), 0))
        same = iota((128, 256), 0) >> 6 == jnp.bitwise_and(iota((128, 256), 1) >> 3, 1)
        for m, a in enumerate((Y, DY)):
            for n, part in enumerate(split(a)):
                W2[128 * n : 128 * n + 128, 256 * m : 256 * m + 256] = (
                    jnp.where(same, dot(part, pick, TN), 0.0).astype(bf16))

    def put(p):
        return pltpu.make_async_copy(FN.at[p], next_ref.at[:, p], out_sem.at[p])

    def place(d):
        return d // 4, pl.ds(2 * lax.rem(d, 4), 2)

    def ccopy(n, peer, slot):
        t, rows = place(peer)
        t2, rows2 = place(slot)
        part = pl.ds(8 * n, 8 - 4 * n)
        return remote(QB.at[part, :, t, rows], CT.at[t2, part, :, rows2], csend.at[n, peer],
                      crecv.at[n, slot], (peer, l, q))

    def send_part(n):
        def add_partner(x, c):
            bcopy(x).wait_recv()
            pair = pl.ds(2 * x, 2)
            QB[pair] = PB[k, pair] + BR[pair]
            return c

        lax.fori_loop(4 * n, 4 + 2 * n, add_partner, 0)
        over(16, g, lambda peer: ccopy(n, peer, g).start())

    def second(j, c):
        wait_halo(j, 1)
        for i, p in enumerate((5 - j, 6 + j)):
            center, add = change(SX, 1, p, 2 * j + i)
            new = 0.5 * (FX[4 + p].reshape(128, 128) + center + add)
            FN[p] = new.reshape(16, 8, 128)
            put(p).start()
        return c

    lax.fori_loop(0, 5, first, 0)
    send_part(0)
    first(5, 0)

    send_part(1)
    projections()

    def ecopy(peer, slot):
        t, rows = place(peer)
        t2, rows2 = place(slot)
        return remote(RB.at[:, :, t, rows], EU.at[:, t2, :, rows2], esend.at[peer], erecv.at[slot],
                      (peer, l, q))

    t, rows = place(g)
    mine = pltpu.make_async_copy(QB.at[:, :, t, rows], CT.at[t, :, :, rows], own_sem.at[0])
    mine.start()
    mine.wait()
    for n in range(2):
        over(16, g, lambda peer: ccopy(n, peer, peer).wait_recv())
    v0 = 8 * (t // 2) + 4 * k + 2 * lax.rem(t, 2)

    def lane_speeds(d):
        which = iota((1, 16), 1)
        pair = [jnp.sum(jnp.where(which == v0 + n, SPD[d : d + 1, :], 0.0), axis=1, keepdims=True)
                for n in range(2)]
        return -0.5 * TIME_STEP * jnp.where(iota((1, 128), 1) < 64, pair[0], pair[1])

    T0, T1 = CT[:, :, 0].reshape(384, 128), CT[:, :, 1].reshape(384, 128)
    R0 = quadrants(dot(X2[...], both(jnp.concatenate([T0, lane_speeds(0) * T1], axis=0))))
    R1 = quadrants(dot(X2[:, 0:384], both(lane_speeds(1) * T1)))
    RB[0] = R0.reshape(6, 4, 8, 128)
    RB[1] = R1.reshape(6, 4, 8, 128)
    over(16, g, lambda peer: ecopy(peer, g).start())

    def send_sections(i, c):
        pl.when(can_send(g, 15, 1))(lambda: xcopy(1, 1, 3 - i).start())
        pl.when(can_send(g, 15, 0))(lambda: xcopy(1, 0, i).start())
        return c

    lax.fori_loop(0, 4, send_sections, 0)
    mine = pltpu.make_async_copy(RB.at[:, :, t, rows], EU.at[:, t, :, rows], own_sem.at[1])
    mine.start()
    mine.wait()
    lax.fori_loop(0, 2, second, 0)
    over(16, g, lambda peer: ecopy(peer, peer).wait_recv())

    def unit(r):
        n = lax.rem(r, 8) - 1
        return 2 * (r // 8) + n // 3, pl.ds(2 * lax.rem(n, 3), 2)

    def working(r):
        return jnp.logical_and(lax.rem(r, 8) >= 1, lax.rem(r, 8) <= 6)

    def fcopy(r):
        t, ranks = unit(r)
        return remote(EU.at[:, t, ranks], FU.at[ring], fsend.at[r], frecv.at[ring], ring_device(r))

    def fcome(r):
        return remote(EU.at[:, 0, pl.ds(0, 2)], FU.at[r], fsend.at[r], frecv.at[r], ring_device(r))

    def send_unit(i, c):
        r = lax.rem(ring + jnp.where(lax.rem(i, 2) == 0, 8 + i // 2, 7 - i // 2), 16)
        pl.when(working(r))(lambda: fcopy(r).start())
        return c

    lax.fori_loop(0, 15, send_unit, 0)
    works = working(ring)

    @pl.when(works)
    def _():
        t, ranks = unit(ring)
        mine = pltpu.make_async_copy(EU.at[:, t, ranks], FU.at[ring], own_sem.at[0])
        mine.start()
        mine.wait()

    def gcopy(there, slot):
        return remote(SB.at[:, there], GB.at[slot], gsend.at[there], grecv.at[slot], (g, there, q))

    lax.fori_loop(2, 6, second, 0)

    @pl.when(works)
    def _():
        over(16, ring, lambda r: fcome(r).wait_recv())
        U = [FU[:, n].reshape(256, 128) for n in range(2)]
        S = quadrants(dot(W2[...], both(jnp.concatenate(U, axis=0))))
        SB[...] = S.reshape(2, 8, 8, 128)
        over(8, l, lambda there: gcopy(there, l - 1).start())
        GB[l - 1] = SB[:, l]

    def done(p, c):
        for s in range(2):
            for d in range(2):
                pl.when(can_send(l, 7, d))(lambda: ycopy(s, d, p).wait_send())
        put(p).wait()
        return c

    lax.fori_loop(0, 12, done, 0)
    for j in range(6):
        bcopy(j).wait_send()
        for d in range(2):
            pl.when(can_send(q, 3, d))(lambda: zcopy(d, j).wait_send())
    for d in range(2):
        pl.when(can_send(q, 3, d))(lambda: z0copy(d).wait_send())
        pl.when(can_send(q, 3, d))(lambda: zfcopy(d).wait_send())
        for s in range(2):
            for i in range(4):
                pl.when(can_send(g, 15, d))(lambda: xcopy(s, d, i).wait_send())

    def done_peer(peer):
        xrow(peer, g).wait_send()
        for n in range(2):
            ccopy(n, peer, g).wait_send()
        ecopy(peer, g).wait_send()

    over(16, g, done_peer)
    over(8, l, lambda peer: yrow(peer, l).wait_send())
    over(16, ring, lambda r: pl.when(working(r))(lambda: fcopy(r).wait_send()))

    for e in range(6):
        pl.when(l != e + 1)(lambda: gcopy(l, e).wait_recv())
    for u in range(2):
        for a in range(6):
            tile = GB[3 * u + a // 2, a % 2]
            core_ref[2 * u, a] = tile[:, 0:54]
            core_ref[2 * u + 1, a] = pltpu.roll(tile, 64, 1)[:, 0:54]

    @pl.when(works)
    def _():
        over(8, l, lambda there: gcopy(there, l - 1).wait_send())


def local(fields, speeds, kinetics, block_rank, x_factor, y_factor, z_factor):
    vmem, dma = pltpu.VMEM, pltpu.SemaphoreType.DMA
    in_vmem = pl.BlockSpec(memory_space=pltpu.VMEM)
    in_hbm = pl.BlockSpec(memory_space=pltpu.HBM)
    return pl.pallas_call(
        kernel,
        out_shape=(
            jax.ShapeDtypeStruct(fields.shape, f32),
            jax.ShapeDtypeStruct((4, 6, 8, 54), f32),
        ),
        in_specs=[in_hbm] * 7,
        out_specs=(in_hbm, in_vmem),
        scratch_shapes=[
            vmem((20, 16, 8, 128), f32),
            vmem((20, 16, 8, 128), f32),
            vmem((2, 12, 16, 8, 128), f32),
            vmem((2, 12, 8, 128), f32),
            vmem((2, 12, 8, 128), f32),
            vmem((12, 16, 8, 128), f32),
            vmem((2, 12, 2, 4, 8, 128), f32),
            vmem((12, 2, 4, 8, 128), f32),
            vmem((12, 2, 4, 8, 128), f32),
            vmem((4, 12, 2, 8, 128), f32),
            vmem((2, 6, 4, 8, 128), f32),
            vmem((2, 4, 6, 8, 128), f32),
            vmem((16, 2, 2, 8, 128), f32),
            vmem((2, 8, 8, 128), f32),
            vmem((6, 2, 8, 128), f32),
            vmem((16, 128), f32),
            vmem((16, 16, 128), f32),
            vmem((8, 128), f32),
            vmem((8, 8, 128), f32),
            vmem((128, 128), f32),
            vmem((8, 128), f32),
            vmem((256, 128), f32),
            vmem((192, 96), f32),
            vmem((8, 64), f32),
            vmem((16, 16), f32),
            vmem((3, 16), f32),
            pltpu.SMEM((12,), jnp.int32),
            vmem((256, 256), bf16),
            vmem((256, 128), bf16),
            vmem((256, 256), bf16),
            vmem((16, 256), bf16),
            vmem((8, 256), bf16),
            vmem((512, 256), bf16),
            vmem((384, 768), bf16),
            vmem((256, 512), bf16),
            vmem((128, 128), f32),
            vmem((128, 128), f32),
            dma((12,)), dma((6,)), dma((12,)), dma((2,)),
            dma((2, 2, 12)), dma((2, 2, 12)),
            dma((2, 6)), dma((2, 6)), dma((2,)), dma((2,)), dma((2,)), dma((2,)),
            dma((2, 2, 4)), dma((2, 2, 4)),
            dma((6,)), dma((6,)),
            dma((2, 16)), dma((2, 16)), dma((16,)), dma((16,)), dma((16,)), dma((16,)),
            dma((8,)), dma((8,)),
            dma((16,)), dma((16,)), dma((8,)), dma((8,)),
            pltpu.SemaphoreType.REGULAR((3,)), pltpu.SemaphoreType.REGULAR((3,)),
        ],
        compiler_params=pltpu.CompilerParams(
            collective_id=0, has_side_effects=True, vmem_limit_bytes=60 * 1024 * 1024),
    )(fields, speeds, kinetics, block_rank, x_factor, y_factor, z_factor.T)


def solution(mesh):
    placed = (P(None, "gx", "gy", "gz"), P(), P(), P("gx"), P(), P("gy", None), P("gz", None))
    return jax.shard_map(
        local,
        mesh=mesh,
        in_specs=placed,
        out_specs=(P(None, "gx", "gy", "gz"), P("gz", "gx", "gy", None)),
        check_vma=False,
    )
```
